128 devices in a mesh: seq: 32 (over x, y, core), chan: 4 (over z).
Axes of the slice: x: 4, y: 4, z: 4, core: 2. Of those that a mesh axis runs over, the one named last changes fastest.
Arguments:
- tokens: bfloat16 [16384, 8192], P('seq', 'chan'), may hold values from -6 to 6
- w_in: bfloat16 [8192, 4096], P('chan'), may hold values from -0.0625 to 0.0625
- gate_k: bfloat16 [16384, 4096], P('seq', 'chan'), may hold values from -6 to 6
- gate_q: bfloat16 [16384, 4096], P('seq', 'chan'), may hold values from -6 to 6
- filters: bfloat16 [16384, 4096], P('seq', 'chan')
- skip: float32 [4096], P('chan'), may hold values from 0.3 to 1.5
Outputs:
- gated: bfloat16 [16384, 4096], P('seq', 'chan')
The draws below stay inside these ranges and needn't reach their ends.
All inputs are finite; a program needn't handle non-finite values.
Results may differ from the reference program's by a relative error of at most 0.009.
Values may be sent and summed in bfloat16 or wider, within the bound.
A program may use at most 192 MiB of HBM per device.

```python
import math
import jax
import jax.numpy as jnp
from jax import lax

D = 8192
CH = 4096
TOKENS = 16384
N_CHAN = 4


def draw_filters(key, part):
    key = jax.random.fold_in(key, 7)
    values = jax.random.normal(key, (TOKENS, CH), jnp.float32)
    return (values * (1.5 / math.sqrt(TOKENS))).astype(jnp.bfloat16)


def block_scale(own_key, shape, cuts, low, high):
    factor_of, own = 1.0, jax.random.fold_in(own_key, 6)
    for axis_at, shards_of in cuts:
        steps = jnp.exp(jax.random.uniform(jax.random.fold_in(own, axis_at), (shards_of,), jnp.float32, low / len(cuts), high / len(cuts)))
        factor_of = factor_of * jnp.repeat(steps, shape[axis_at] // shards_of).reshape([-1 if axis == axis_at else 1 for axis in range(len(shape))])
    return factor_of


def scatter_about(rng, shape, scale, limit, split=(), dtype=jnp.bfloat16):
    entries = scale * jax.random.normal(rng, shape, jnp.float32)
    if split:
        entries = entries * block_scale(rng, shape, split, -0.22, 0.18)
    return jnp.clip(entries, -limit, limit).astype(dtype)


def setup_inputs(seed: int = 0) -> dict:
    splits = jax.random.split(jax.random.key(seed), 7)
    return {
        "tokens": scatter_about(splits[0], (TOKENS, D), 1.0, 6.0, ((0, 32), (1, 4))),
        "w_in": scatter_about(splits[1], (D, CH), D ** -0.5, 0.0625, ((0, 4),)),
        "gate_k": scatter_about(splits[2], (TOKENS, CH), 1.0, 6.0, ((0, 32), (1, 4))),
        "gate_q": scatter_about(splits[3], (TOKENS, CH), 1.0, 6.0, ((0, 32), (1, 4))),
        "filters": draw_filters(jax.random.fold_in(splits[6], 71), 0),
        "skip": jnp.clip(jnp.exp(math.log(1.5) - 1.60943787 * jax.random.uniform(splits[5], (CH,), jnp.float32) ** block_scale(splits[5], (CH,), ((0, 4),), -0.2, 0.2)), 0.3, 1.5),
    }


def spectral(operands):
    values, responses = operands
    value_freq = jnp.fft.rfft(values, n=2 * TOKENS, axis=0)
    filter_freq = jnp.fft.rfft(responses, n=2 * TOKENS, axis=0)
    return jnp.fft.irfft(value_freq * filter_freq, n=2 * TOKENS, axis=0)[:TOKENS]


def reference(tokens, w_in, gate_k, gate_q, filters, skip):
    value = jnp.dot(tokens, w_in, preferred_element_type=jnp.float32)
    mixed = (gate_k.astype(jnp.float32) * value).astype(jnp.bfloat16)
    group_width = CH // N_CHAN

    def regroup(array):
        return array.astype(jnp.float32).reshape(TOKENS, N_CHAN, group_width).transpose(1, 0, 2)

    conv = lax.map(spectral, (regroup(mixed), regroup(filters)))
    conv = conv.astype(jnp.float32).transpose(1, 0, 2).reshape(TOKENS, CH)
    result = gate_q.astype(jnp.float32) * (conv + skip[None, :] * mixed.astype(jnp.float32))
    return result.astype(jnp.bfloat16)
```

```python
import math

import jax
import jax.numpy as jnp
import numpy as np
from jax import lax
from jax.experimental import pallas as pl
from jax.experimental.pallas import tpu as pltpu
from jax.sharding import PartitionSpec as P

MESH = pl.DeviceIdType.MESH
SEQ = 32
CHAN = 4
ROWS = 512
FEAT = 2048
WIDTH = 1024
N1 = 128
OWN_A = ROWS // N1
NC = 4
CW = WIDTH // NC
CD = CW // SEQ
BR = OWN_A * CD
HALF = ROWS // 2
F32, BF16 = jnp.float32, jnp.bfloat16


def tables():
    n = N1 * N1
    k = np.arange(N1, dtype=np.float64)
    first = 2.0 * math.pi / N1 * np.outer(k + 0.25, k)
    fwd = np.concatenate([np.cos(first), -np.sin(first)], 0)
    inv = fwd.T / n
    turn = 2.0 * math.pi / n * np.outer(k + 0.25, k)
    tw = np.stack([np.cos(turn), -np.sin(turn)])
    second = 2.0 * math.pi / N1 * np.outer(k, k)
    c, s = np.cos(second), np.sin(second)
    mid = np.block([[c, -s], [s, c]])
    mid_inv = np.block([[c, s], [-s, c]])
    bf = [jnp.asarray(m, F32).astype(BF16) for m in (fwd, mid, mid_inv, inv)]
    return (*bf, jnp.asarray(tw, F32))


def kernel(
    tok_hbm, w_hbm, gk_hbm, gq_hbm, fl_hbm, skip_hbm, fwd_hbm, mid_hbm, midi_hbm, inv_hbm, tw_hbm,
    out_hbm,
    tok, wbuf, wown, gk, gq, fl, skip, fwd, mid, midi, inv, tw,
    z2s, z2r, pa, zs, zr, own, mixed, out,
    fs, fr, xs, xr, ys, yr, bounce, lanes, spec,
    in_sem, w_sem, wown_sem, out_sem,
    z2s_sem, z2r_sem, zs_sem, zr_sem, fs_sem, fr_sem, xs_sem, xr_sem, ys_sem, yr_sem,
):
    s, c = lax.axis_index("seq"), lax.axis_index("chan")
    up, down, far = lax.rem(c + 1, CHAN), lax.rem(c + 3, CHAN), lax.rem(c + 2, CHAN)
    ex, why, core = s // 8, lax.rem(s // 2, 4), lax.rem(s, 2)
    owners = (far, up, down)

    def plane_each(body):
        def step(m, carry):
            q = lax.rem(11 * m, 16)
            chip = lax.rem(ex + q // 4, 4) * 4 + lax.rem(why + lax.rem(q, 4), 4)
            body(chip * 2 + core)
            body(chip * 2 + 1 - core)
            return carry

        lax.fori_loop(1, 16, step, 0)
        body(s + 1 - 2 * core)

    loads = [
        pltpu.make_async_copy(a, b, in_sem.at[i])
        for i, (a, b) in enumerate(
            [(tok_hbm, tok), (gk_hbm, gk), (gq_hbm, gq), (fl_hbm, fl), (skip_hbm, skip), (fwd_hbm, fwd),
             (mid_hbm, mid), (midi_hbm, midi), (inv_hbm, inv), (tw_hbm, tw)]
        )
    ]

    def w_copy(kind, j):
        col = pl.multiple_of(owners[kind] * WIDTH + j * CW, CW)
        slot = lax.rem(j, 2)
        return pltpu.make_async_copy(
            w_hbm.at[:, pl.ds(col, CW)], wbuf.at[kind, slot], w_sem.at[kind, slot]
        )

    def wown_copy(j):
        col = pl.multiple_of(c * WIDTH + j * CW, CW)
        return pltpu.make_async_copy(w_hbm.at[:, pl.ds(col, CW)], wown.at[j], wown_sem.at[j])

    loads[0].start()
    for kind in range(3):
        w_copy(kind, 0).start()
    loads[3].start()
    for kind in range(3):
        w_copy(kind, 1).start()
    for i in (1, 2, 4, 5, 6, 7, 8, 9):
        loads[i].start()
    for j in range(NC):
        wown_copy(j).start()

    barrier = pltpu.get_barrier_semaphore()
    for z in (up, down):
        pl.semaphore_signal(barrier, inc=1, device_id=(s, z), device_id_type=MESH)
    plane_each(
        lambda d: pl.semaphore_signal(barrier, inc=1, device_id=(d, c), device_id_type=MESH)
    )

    loads[0].wait()
    loads[3].wait()

    def z2_copy(j, half):
        rows = pl.ds(half * HALF, HALF)
        return pltpu.make_async_remote_copy(
            z2s.at[j, rows], z2r.at[j, rows], z2s_sem.at[j, half], z2r_sem.at[j, half],
            device_id=(s, (up, down)[half]), device_id_type=MESH,
        )

    def z_copy(j, way):
        return pltpu.make_async_remote_copy(
            zs.at[way, j], zr.at[way, j], zs_sem.at[way, j], zr_sem.at[way, j],
            device_id=(s, (up, down)[way]), device_id_type=MESH,
        )

    def plane_send(src, dst, send_sem, recv_sem, j):
        def one(d):
            pltpu.make_async_remote_copy(
                src.at[j, d], dst.at[j, s], send_sem.at[j], recv_sem.at[j],
                device_id=(d, c), device_id_type=MESH,
            ).start()

        plane_each(one)
        dst[j, s] = src[j, s]

    def plane_wait(src, dst, send_sem, recv_sem, j):
        return pltpu.make_async_remote_copy(
            src.at[j, pl.ds(0, SEQ - 1)], dst.at[j, pl.ds(0, SEQ - 1)],
            send_sem.at[j], recv_sem.at[j], device_id=(s, c), device_id_type=MESH,
        )

    def to_blocks(values, dst, j):
        for a in range(OWN_A):
            part = values[a * N1 : (a + 1) * N1].T.reshape(SEQ, CD, N1)
            bounce[:, a * CD : (a + 1) * CD, :] = part
        dst[j] = bounce[...].astype(BF16)

    def chunk(j):
        return pl.ds(pl.multiple_of(j * CW, CW), CW)

    def finish(j):
        for way in range(2):
            z2_copy(j, way).wait_recv()
            rows = pl.ds(way * HALF, HALF)
            zs[way, j, rows] = (pa[way, j] + z2r[j, rows].astype(F32)).astype(BF16)
            z_copy(j, way).start()

    def project(j, carry):
        for kind in range(3):
            slot = lax.rem(j, 2)
            w_copy(kind, j).wait()
            part = jnp.dot(tok[...], wbuf[kind, slot], preferred_element_type=F32)
            if kind == 0:
                z2s[j] = part.astype(BF16)

                @pl.when(j == 0)
                def _():
                    pl.semaphore_wait(barrier, SEQ + 1)

                z2_copy(j, 0).start()
                z2_copy(j, 1).start()
            else:
                way = kind - 1
                other = 1 - way
                pa[way, j] = part[way * HALF : (way + 1) * HALF]
                zs[way, j, pl.ds(other * HALF, HALF)] = part[
                    other * HALF : (other + 1) * HALF
                ].astype(BF16)

            @pl.when(j + 2 < NC)
            def _():
                w_copy(kind, j + 2).start()

        to_blocks(fl[:, chunk(j)].astype(F32), fs, j)
        plane_send(fs, fr, fs_sem, fr_sem, j)

        @pl.when(j > 0)
        def _():
            finish(j - 1)

        return carry

    lax.fori_loop(0, NC, project, 0)
    finish(NC - 1)

    def project_own(j, carry):
        wown_copy(j).wait()
        own[j] = jnp.dot(tok[...], wown[j], preferred_element_type=F32)
        return carry

    lax.fori_loop(0, NC, project_own, 0)
    for i in (1, 2, 4, 5, 6, 7, 8, 9):
        loads[i].wait()

    def forward(i):
        pair = jnp.concatenate(
            [lanes[pl.ds(i, N1, stride=CD), :], lanes[pl.ds(i + 1, N1, stride=CD), :]], axis=1
        ).astype(BF16)
        first = jnp.dot(fwd[...], pair, preferred_element_type=F32)
        rows = []
        for q in range(2):
            re = first[:N1, q * N1 : (q + 1) * N1]
            im = first[N1:, q * N1 : (q + 1) * N1]
            rows.append(
                jnp.concatenate([re * tw[0] - im * tw[1], re * tw[1] + im * tw[0]], axis=1)
            )
        turned = jnp.concatenate(rows, axis=0).astype(BF16)
        return jnp.dot(turned, mid[...], preferred_element_type=F32)

    def load_lanes(src, j):
        lanes[...] = src[j].astype(F32).reshape(SEQ * BR, N1)

    def transform_filters(j, carry):
        plane_wait(fs, fr, fs_sem, fr_sem, j).wait_recv()
        load_lanes(fr, j)
        for p in range(CD // 2):
            spec[j, p] = forward(2 * p)
        return carry

    lax.fori_loop(0, NC, transform_filters, 0)

    def gather_sums(j):
        z_copy(j, 0).wait_recv()
        z_copy(j, 1).wait_recv()
        value = own[j] + zr[0, j].astype(F32) + zr[1, j].astype(F32)
        mix = (gk[:, chunk(j)].astype(F32) * value).astype(BF16)
        mixed[:, chunk(j)] = mix
        to_blocks(mix.astype(F32), xs, j)
        plane_send(xs, xr, xs_sem, xr_sem, j)

    def convolve(j):
        plane_wait(xs, xr, xs_sem, xr_sem, j).wait_recv()
        load_lanes(xr, j)
        for p in range(CD // 2):
            freq = forward(2 * p)
            filt = spec[j, p]
            re, im = freq[:, :N1], freq[:, N1:]
            fre, fim = filt[:, :N1], filt[:, N1:]
            prod = jnp.concatenate([re * fre - im * fim, re * fim + im * fre], axis=1)
            back = jnp.dot(prod.astype(BF16), midi[...], preferred_element_type=F32)
            tops, bottoms = [], []
            for q in range(2):
                bre = back[q * N1 : (q + 1) * N1, :N1]
                bim = back[q * N1 : (q + 1) * N1, N1:]
                tops.append(bre * tw[0] + bim * tw[1])
                bottoms.append(bim * tw[0] - bre * tw[1])
            turned = jnp.concatenate(
                [jnp.concatenate(tops, axis=1), jnp.concatenate(bottoms, axis=1)], axis=0
            ).astype(BF16)
            conv = jnp.dot(inv[...], turned, preferred_element_type=F32)
            lanes[pl.ds(2 * p, N1, stride=CD), :] = conv[:, :N1]
            lanes[pl.ds(2 * p + 1, N1, stride=CD), :] = conv[:, N1:]
        ys[j] = lanes[...].reshape(SEQ, BR, N1).astype(BF16)
        plane_send(ys, yr, ys_sem, yr_sem, j)

    def out_copy(j):
        return pltpu.make_async_copy(out.at[:, chunk(j)], out_hbm.at[:, chunk(j)], out_sem.at[j])

    def finalize(j):
        plane_wait(ys, yr, ys_sem, yr_sem, j).wait_recv()
        bounce[...] = yr[j].astype(F32)
        for a in range(OWN_A):
            conv = bounce[:, a * CD : (a + 1) * CD, :].reshape(CW, N1).T
            rows = pl.ds(a * N1, N1)
            total = conv + skip[:, chunk(j)] * mixed[rows, chunk(j)].astype(F32)
            out[rows, chunk(j)] = (gq[rows, chunk(j)].astype(F32) * total).astype(BF16)
        out_copy(j).start()

    def pipeline(j, carry):
        @pl.when(j < NC)
        def _():
            gather_sums(j)

        @pl.when(jnp.logical_and(j >= 1, j <= NC))
        def _():
            convolve(j - 1)

        @pl.when(j >= 2)
        def _():
            finalize(j - 2)

        return carry

    lax.fori_loop(0, NC + 2, pipeline, 0)

    def drain(j, carry):
        out_copy(j).wait()
        for way in range(2):
            z2_copy(j, way).wait_send()
            z_copy(j, way).wait_send()
        plane_wait(fs, fr, fs_sem, fr_sem, j).wait_send()
        plane_wait(xs, xr, xs_sem, xr_sem, j).wait_send()
        plane_wait(ys, yr, ys_sem, yr_sem, j).wait_send()
        return carry

    lax.fori_loop(0, NC, drain, 0)


def local(tokens, w_in, gate_k, gate_q, filters, skip):
    any_spec = pl.BlockSpec(memory_space=pl.ANY)
    vm = pltpu.VMEM
    dma = pltpu.SemaphoreType.DMA
    block = (NC, SEQ, BR, N1)
    scratch = [
        vm((ROWS, FEAT), BF16), vm((3, 2, FEAT, CW), BF16), vm((NC, FEAT, CW), BF16),
        vm((ROWS, WIDTH), BF16), vm((ROWS, WIDTH), BF16), vm((ROWS, WIDTH), BF16), vm((1, WIDTH), F32),
        vm((2 * N1, N1), BF16), vm((2 * N1, 2 * N1), BF16), vm((2 * N1, 2 * N1), BF16),
        vm((N1, 2 * N1), BF16), vm((2, N1, N1), F32),
        vm((NC, ROWS, CW), BF16), vm((NC, ROWS, CW), BF16), vm((2, NC, HALF, CW), F32),
        vm((2, NC, ROWS, CW), BF16), vm((2, NC, ROWS, CW), BF16), vm((NC, ROWS, CW), F32),
        vm((ROWS, WIDTH), BF16), vm((ROWS, WIDTH), BF16),
        vm(block, BF16), vm(block, BF16), vm(block, BF16), vm(block, BF16), vm(block, BF16), vm(block, BF16),
        vm((SEQ, BR, N1), F32), vm((SEQ * BR, N1), F32), vm((NC, CD // 2, 2 * N1, 2 * N1), F32),
        dma((10,)), dma((3, 2)), dma((NC,)), dma((NC,)),
        dma((NC, 2)), dma((NC, 2)), dma((2, NC)), dma((2, NC)),
        dma((NC,)), dma((NC,)), dma((NC,)), dma((NC,)), dma((NC,)), dma((NC,)),
    ]
    return pl.pallas_call(
        kernel,
        out_shape=jax.ShapeDtypeStruct((ROWS, WIDTH), BF16),
        in_specs=[any_spec] * 11,
        out_specs=any_spec,
        scratch_shapes=scratch,
        compiler_params=pltpu.CompilerParams(
            collective_id=0, has_side_effects=True, vmem_limit_bytes=60 * 2**20
        ),
        name="hyena_block",
    )(tokens, w_in, gate_k, gate_q, filters, skip.reshape(1, WIDTH), *tables())


def solution(mesh):
    in_specs = (
        P("seq", "chan"),
        P("chan", None),
        P("seq", "chan"),
        P("seq", "chan"),
        P("seq", "chan"),
        P("chan"),
    )
    out_specs = P("seq", "chan")
    return jax.shard_map(local, mesh=mesh, in_specs=in_specs, out_specs=out_specs, check_vma=False)
```

```python
import math

import jax
import jax.numpy as jnp
import numpy as np
from jax import lax
from jax.experimental import pallas as pl
from jax.experimental.pallas import tpu as pltpu
from jax.sharding import PartitionSpec as P

MESH = pl.DeviceIdType.MESH
SEQ = 32
CHAN = 4
ROWS = 512
FEAT = 2048
WIDTH = 1024
N1 = 128
OWN_A = ROWS // N1
NC = 4
CW = WIDTH // NC
CD = CW // SEQ
BR = OWN_A * CD
HALF = ROWS // 2
F32, BF16 = jnp.float32, jnp.bfloat16


def tables():
    n = N1 * N1
    k = np.arange(N1, dtype=np.float64)
    first = 2.0 * math.pi / N1 * np.outer(k + 0.25, k)
    fwd = np.concatenate([np.cos(first), -np.sin(first)], 0)
    inv = fwd.T / n
    turn = 2.0 * math.pi / n * np.outer(k + 0.25, k)
    tw = np.stack([np.cos(turn), -np.sin(turn)])
    second = 2.0 * math.pi / N1 * np.outer(k, k)
    c, s = np.cos(second), np.sin(second)
    mid = np.block([[c, -s], [s, c]])
    mid_inv = np.block([[c, s], [-s, c]])
    bf = [jnp.asarray(m, F32).astype(BF16) for m in (fwd, mid, mid_inv, inv)]
    return (*bf, jnp.asarray(tw, F32))


def kernel(
    tok_hbm, w_hbm, gk_hbm, gq_hbm, fl_hbm, skip_hbm, fwd_hbm, mid_hbm, midi_hbm, inv_hbm, tw_hbm,
    out_hbm,
    tok, wbuf, wown, gk, gq, fl, skip, fwd, mid, midi, inv, tw,
    z2s, z2r, zs, zr, own, mixed, out,
    fs, fr, xs, xr, ys, yr, bounce, lanes, spec,
    in_sem, w_sem, wown_sem, out_sem,
    z2s_sem, z2r_sem, zs_sem, zr_sem, fs_sem, fr_sem, xs_sem, xr_sem, ys_sem, yr_sem,
):
    s, c = lax.axis_index("seq"), lax.axis_index("chan")
    up, down, far = lax.rem(c + 1, CHAN), lax.rem(c + 3, CHAN), lax.rem(c + 2, CHAN)
    ex, why, core = s // 8, lax.rem(s // 2, 4), lax.rem(s, 2)
    owners = (far, up, down)

    def plane_each(body):
        def step(m, carry):
            q = lax.rem(11 * m, 16)
            chip = lax.rem(ex + q // 4, 4) * 4 + lax.rem(why + lax.rem(q, 4), 4)
            body(chip * 2 + core)
            body(chip * 2 + 1 - core)
            return carry

        lax.fori_loop(1, 16, step, 0)
        body(s + 1 - 2 * core)

    loads = [
        pltpu.make_async_copy(a, b, in_sem.at[i])
        for i, (a, b) in enumerate(
            [(tok_hbm, tok), (gk_hbm, gk), (gq_hbm, gq), (fl_hbm, fl), (skip_hbm, skip), (fwd_hbm, fwd),
             (mid_hbm, mid), (midi_hbm, midi), (inv_hbm, inv), (tw_hbm, tw)]
        )
    ]

    def w_copy(kind, j):
        col = pl.multiple_of(owners[kind] * WIDTH + j * CW, CW)
        slot = lax.rem(j, 2)
        return pltpu.make_async_copy(
            w_hbm.at[:, pl.ds(col, CW)], wbuf.at[kind, slot], w_sem.at[kind, slot]
        )

    def wown_copy(j):
        col = pl.multiple_of(c * WIDTH + j * CW, CW)
        return pltpu.make_async_copy(w_hbm.at[:, pl.ds(col, CW)], wown.at[j], wown_sem.at[j])

    loads[0].start()
    for kind in range(3):
        w_copy(kind, 0).start()
    loads[3].start()
    for kind in range(3):
        w_copy(kind, 1).start()
    for i in (1, 2, 4, 5, 6, 7, 8, 9):
        loads[i].start()
    for j in range(NC):
        wown_copy(j).start()

    barrier = pltpu.get_barrier_semaphore()
    for z in (up, down):
        pl.semaphore_signal(barrier, inc=1, device_id=(s, z), device_id_type=MESH)
    plane_each(
        lambda d: pl.semaphore_signal(barrier, inc=1, device_id=(d, c), device_id_type=MESH)
    )

    loads[0].wait()
    loads[3].wait()

    def z2_copy(j, half):
        rows = pl.ds(half * HALF, HALF)
        return pltpu.make_async_remote_copy(
            z2s.at[j, rows], z2r.at[j, rows], z2s_sem.at[j, half], z2r_sem.at[j, half],
            device_id=(s, (up, down)[half]), device_id_type=MESH,
        )

    def z_copy(j, way):
        return pltpu.make_async_remote_copy(
            zs.at[way, j], zr.at[way, j], zs_sem.at[way, j], zr_sem.at[way, j],
            device_id=(s, (up, down)[way]), device_id_type=MESH,
        )

    def plane_send(src, dst, send_sem, recv_sem, j):
        def one(d):
            pltpu.make_async_remote_copy(
                src.at[j, d], dst.at[j, s], send_sem.at[j], recv_sem.at[j],
                device_id=(d, c), device_id_type=MESH,
            ).start()

        plane_each(one)
        dst[j, s] = src[j, s]

    def plane_wait(src, dst, send_sem, recv_sem, j):
        return pltpu.make_async_remote_copy(
            src.at[j, pl.ds(0, SEQ - 1)], dst.at[j, pl.ds(0, SEQ - 1)],
            send_sem.at[j], recv_sem.at[j], device_id=(s, c), device_id_type=MESH,
        )

    def to_blocks(values, dst, j):
        for a in range(OWN_A):
            part = values[a * N1 : (a + 1) * N1].T.reshape(SEQ, CD, N1)
            bounce[:, a * CD : (a + 1) * CD, :] = part
        dst[j] = bounce[...].astype(BF16)

    def chunk(j):
        return pl.ds(pl.multiple_of(j * CW, CW), CW)

    def project(kind, j):
        slot = lax.rem(j, 2)
        w_copy(kind, j).wait()
        part = jnp.dot(tok[...], wbuf[kind, slot], preferred_element_type=F32)

        @pl.when(j + 2 < NC)
        def _():
            w_copy(kind, j + 2).start()

        return part

    def project_far(j, carry):
        z2s[j] = project(0, j).astype(BF16)

        @pl.when(j == 0)
        def _():
            pl.semaphore_wait(barrier, SEQ + 1)

        z2_copy(j, 0).start()
        z2_copy(j, 1).start()
        return carry

    def project_near(j, carry):
        for way in range(2):
            part = project(1 + way, j)
            mine, other = pl.ds(way * HALF, HALF), pl.ds((1 - way) * HALF, HALF)
            z2_copy(j, way).wait_recv()
            zs[way, j, other] = part[(1 - way) * HALF : (2 - way) * HALF].astype(BF16)
            zs[way, j, mine] = (
                part[way * HALF : (way + 1) * HALF] + z2r[j, mine].astype(F32)
            ).astype(BF16)
            z_copy(j, way).start()
        return carry

    def project_own(j, carry):
        wown_copy(j).wait()
        own[j] = jnp.dot(tok[...], wown[j], preferred_element_type=F32)
        return carry

    def block_filters(j, carry):
        to_blocks(fl[:, chunk(j)].astype(F32), fs, (0, slice(None), pl.ds(pl.multiple_of(j * BR, BR), BR)))
        return carry

    lax.fori_loop(0, NC, project_far, 0)
    lax.fori_loop(0, NC, block_filters, 0)
    plane_send(fs, fr, fs_sem, fr_sem, 0)
    lax.fori_loop(0, NC, project_near, 0)
    lax.fori_loop(0, NC, project_own, 0)
    for i in (1, 2, 4, 5, 6, 7, 8, 9):
        loads[i].wait()

    def forward(i):
        pair = jnp.concatenate(
            [lanes[pl.ds(i, N1, stride=CD), :], lanes[pl.ds(i + 1, N1, stride=CD), :]], axis=1
        ).astype(BF16)
        first = jnp.dot(fwd[...], pair, preferred_element_type=F32)
        rows = []
        for q in range(2):
            re = first[:N1, q * N1 : (q + 1) * N1]
            im = first[N1:, q * N1 : (q + 1) * N1]
            rows.append(
                jnp.concatenate([re * tw[0] - im * tw[1], re * tw[1] + im * tw[0]], axis=1)
            )
        turned = jnp.concatenate(rows, axis=0).astype(BF16)
        return jnp.dot(turned, mid[...], preferred_element_type=F32)

    def load_lanes(src, j):
        lanes[...] = src[j].astype(F32).reshape(SEQ * BR, N1)

    def transform_filters(j, carry):
        load_lanes(fr, (0, slice(None), pl.ds(pl.multiple_of(j * BR, BR), BR)))
        for p in range(CD // 2):
            spec[j, p] = forward(2 * p)
        return carry

    plane_wait(fs, fr, fs_sem, fr_sem, 0).wait_recv()
    transform_filters(0, 0)

    def gather_sums(j):
        z_copy(j, 0).wait_recv()
        z_copy(j, 1).wait_recv()
        value = own[j] + zr[0, j].astype(F32) + zr[1, j].astype(F32)
        mix = (gk[:, chunk(j)].astype(F32) * value).astype(BF16)
        mixed[:, chunk(j)] = mix
        to_blocks(mix.astype(F32), xs, j)
        plane_send(xs, xr, xs_sem, xr_sem, j)

    def convolve(j):
        plane_wait(xs, xr, xs_sem, xr_sem, j).wait_recv()
        load_lanes(xr, j)
        for p in range(CD // 2):
            freq = forward(2 * p)
            filt = spec[j, p]
            re, im = freq[:, :N1], freq[:, N1:]
            fre, fim = filt[:, :N1], filt[:, N1:]
            prod = jnp.concatenate([re * fre - im * fim, re * fim + im * fre], axis=1)
            back = jnp.dot(prod.astype(BF16), midi[...], preferred_element_type=F32)
            tops, bottoms = [], []
            for q in range(2):
                bre = back[q * N1 : (q + 1) * N1, :N1]
                bim = back[q * N1 : (q + 1) * N1, N1:]
                tops.append(bre * tw[0] + bim * tw[1])
                bottoms.append(bim * tw[0] - bre * tw[1])
            turned = jnp.concatenate(
                [jnp.concatenate(tops, axis=1), jnp.concatenate(bottoms, axis=1)], axis=0
            ).astype(BF16)
            conv = jnp.dot(inv[...], turned, preferred_element_type=F32)
            lanes[pl.ds(2 * p, N1, stride=CD), :] = conv[:, :N1]
            lanes[pl.ds(2 * p + 1, N1, stride=CD), :] = conv[:, N1:]
        ys[j] = lanes[...].reshape(SEQ, BR, N1).astype(BF16)
        plane_send(ys, yr, ys_sem, yr_sem, j)

    def out_copy(j):
        return pltpu.make_async_copy(out.at[:, chunk(j)], out_hbm.at[:, chunk(j)], out_sem.at[j])

    def finalize(j):
        plane_wait(ys, yr, ys_sem, yr_sem, j).wait_recv()
        bounce[...] = yr[j].astype(F32)
        for a in range(OWN_A):
            conv = bounce[:, a * CD : (a + 1) * CD, :].reshape(CW, N1).T
            rows = pl.ds(a * N1, N1)
            total = conv + skip[:, chunk(j)] * mixed[rows, chunk(j)].astype(F32)
            out[rows, chunk(j)] = (gq[rows, chunk(j)].astype(F32) * total).astype(BF16)
        out_copy(j).start()

    def pipeline(j, carry):
        gather_sums(j)

        @pl.when(j == 0)
        def _():
            lax.fori_loop(1, NC, transform_filters, 0)

        @pl.when(j >= 1)
        def _():
            convolve(j - 1)

        return carry

    def finish(j, carry):
        finalize(j)
        return carry

    lax.fori_loop(0, NC, pipeline, 0)
    lax.fori_loop(0, NC - 2, finish, 0)
    convolve(NC - 1)
    lax.fori_loop(NC - 2, NC, finish, 0)

    def drain(j, carry):
        out_copy(j).wait()
        for way in range(2):
            z2_copy(j, way).wait_send()
            z_copy(j, way).wait_send()
        plane_wait(xs, xr, xs_sem, xr_sem, j).wait_send()
        plane_wait(ys, yr, ys_sem, yr_sem, j).wait_send()
        return carry

    plane_wait(fs, fr, fs_sem, fr_sem, 0).wait_send()
    lax.fori_loop(0, NC, drain, 0)


def local(tokens, w_in, gate_k, gate_q, filters, skip):
    any_spec = pl.BlockSpec(memory_space=pl.ANY)
    vm = pltpu.VMEM
    dma = pltpu.SemaphoreType.DMA
    block = (NC, SEQ, BR, N1)
    scratch = [
        vm((ROWS, FEAT), BF16), vm((3, 2, FEAT, CW), BF16), vm((NC, FEAT, CW), BF16),
        vm((ROWS, WIDTH), BF16), vm((ROWS, WIDTH), BF16), vm((ROWS, WIDTH), BF16), vm((1, WIDTH), F32),
        vm((2 * N1, N1), BF16), vm((2 * N1, 2 * N1), BF16), vm((2 * N1, 2 * N1), BF16),
        vm((N1, 2 * N1), BF16), vm((2, N1, N1), F32),
        vm((NC, ROWS, CW), BF16), vm((NC, ROWS, CW), BF16),
        vm((2, NC, ROWS, CW), BF16), vm((2, NC, ROWS, CW), BF16), vm((NC, ROWS, CW), F32),
        vm((ROWS, WIDTH), BF16), vm((ROWS, WIDTH), BF16),
        vm((1, SEQ, NC * BR, N1), BF16), vm((1, SEQ, NC * BR, N1), BF16),
        vm(block, BF16), vm(block, BF16), vm(block, BF16), vm(block, BF16),
        vm((SEQ, BR, N1), F32), vm((SEQ * BR, N1), F32), vm((NC, CD // 2, 2 * N1, 2 * N1), F32),
        dma((10,)), dma((3, 2)), dma((NC,)), dma((NC,)),
        dma((NC, 2)), dma((NC, 2)), dma((2, NC)), dma((2, NC)),
        dma((1,)), dma((1,)), dma((NC,)), dma((NC,)), dma((NC,)), dma((NC,)),
    ]
    return pl.pallas_call(
        kernel,
        out_shape=jax.ShapeDtypeStruct((ROWS, WIDTH), BF16),
        in_specs=[any_spec] * 11,
        out_specs=any_spec,
        scratch_shapes=scratch,
        compiler_params=pltpu.CompilerParams(
            collective_id=0, has_side_effects=True, vmem_limit_bytes=60 * 2**20
        ),
        name="hyena_block",
    )(tokens, w_in, gate_k, gate_q, filters, skip.reshape(1, WIDTH), *tables())


def solution(mesh):
    in_specs = (
        P("seq", "chan"),
        P("chan", None),
        P("seq", "chan"),
        P("seq", "chan"),
        P("seq", "chan"),
        P("chan"),
    )
    out_specs = P("seq", "chan")
    return jax.shard_map(local, mesh=mesh, in_specs=in_specs, out_specs=out_specs, check_vma=False)
```

```python
import math

import jax
import jax.numpy as jnp
import numpy as np
from jax import lax
from jax.experimental import pallas as pl
from jax.experimental.pallas import tpu as pltpu
from jax.sharding import PartitionSpec as P

MESH = pl.DeviceIdType.MESH
SEQ = 32
CHAN = 4
ROWS = 512
FEAT = 2048
WIDTH = 1024
N1 = 128
OWN_A = ROWS // N1
NC = 4
CW = WIDTH // NC
CD = CW // SEQ
BR = OWN_A * CD
HALF = ROWS // 2
F32, BF16 = jnp.float32, jnp.bfloat16


def tables():
    n = N1 * N1
    k = np.arange(N1, dtype=np.float64)
    first = 2.0 * math.pi / N1 * np.outer(k + 0.25, k)
    fwd = np.concatenate([np.cos(first), -np.sin(first)], 0)
    inv = fwd.T / n
    turn = 2.0 * math.pi / n * np.outer(k + 0.25, k)
    tw = np.stack([np.cos(turn), -np.sin(turn)])
    second = 2.0 * math.pi / N1 * np.outer(k, k)
    c, s = np.cos(second), np.sin(second)
    mid = np.block([[c, -s], [s, c]])
    mid_inv = np.block([[c, s], [-s, c]])
    bf = [jnp.asarray(m, F32).astype(BF16) for m in (fwd, mid, mid_inv, inv)]
    return (*bf, jnp.asarray(tw, F32))


def kernel(
    tok_hbm, w_hbm, gk_hbm, gq_hbm, fl_hbm, skip_hbm, fwd_hbm, mid_hbm, midi_hbm, inv_hbm, tw_hbm,
    out_hbm,
    tok, wfar, wnear, wown, gk, gq, fl, skip, fwd, mid, midi, inv, tw,
    z2s, z2r, zs, zr, own, mixed, out,
    fs, fr, xs, xr, ys, yr, bounce, lanes, turns, spec, pos, first, rows, second, back,
    in_sem, wfar_sem, wnear_sem, wown_sem, out_sem,
    z2s_sem, z2r_sem, zs_sem, zr_sem, fs_sem, fr_sem, xs_sem, xr_sem, ys_sem, yr_sem,
):
    s, c = lax.axis_index("seq"), lax.axis_index("chan")
    up, down, far = lax.rem(c + 1, CHAN), lax.rem(c + 3, CHAN), lax.rem(c + 2, CHAN)
    ex, why, core = s // 8, lax.rem(s // 2, 4), lax.rem(s, 2)

    def plane_each(body):
        def step(m, carry):
            q = lax.rem(11 * m, 16)
            chip = lax.rem(ex + q // 4, 4) * 4 + lax.rem(why + lax.rem(q, 4), 4)
            body(chip * 2 + core)
            body(chip * 2 + 1 - core)
            return carry

        lax.fori_loop(1, 16, step, 0)
        body(s + 1 - 2 * core)

    loads = [
        pltpu.make_async_copy(a, b, in_sem.at[i])
        for i, (a, b) in enumerate(
            [(tok_hbm, tok), (gk_hbm, gk), (gq_hbm, gq), (fl_hbm, fl), (skip_hbm, skip), (fwd_hbm, fwd),
             (mid_hbm, mid), (midi_hbm, midi), (inv_hbm, inv), (tw_hbm, tw)]
        )
    ]

    def w_copy(owner, j, dst, sem):
        col = pl.multiple_of(owner * WIDTH + j * CW, CW)
        return pltpu.make_async_copy(w_hbm.at[:, pl.ds(col, CW)], dst, sem)

    def far_copy(j):
        return w_copy(far, j, wfar.at[j], wfar_sem.at[j])

    def near_copy(way, j):
        slot = lax.rem(j, 2)
        return w_copy((up, down)[way], j, wnear.at[way, slot], wnear_sem.at[way, slot])

    def own_copy(j):
        return w_copy(c, j, wown.at[j], wown_sem.at[j])

    loads[0].start()
    far_copy(0).start()

    barrier = pltpu.get_barrier_semaphore()
    for z in (up, down):
        pl.semaphore_signal(barrier, inc=1, device_id=(s, z), device_id_type=MESH)
    plane_each(
        lambda d: pl.semaphore_signal(barrier, inc=1, device_id=(d, c), device_id_type=MESH)
    )

    loads[0].wait()
    far_copy(0).wait()
    for j in range(1, NC):
        far_copy(j).start()

    def z2_copy(j, half):
        half_rows = pl.ds(half * HALF, HALF)
        return pltpu.make_async_remote_copy(
            z2s.at[j, half_rows], z2r.at[j, half_rows], z2s_sem.at[j, half], z2r_sem.at[j, half],
            device_id=(s, (up, down)[half]), device_id_type=MESH,
        )

    def z_copy(j, way):
        return pltpu.make_async_remote_copy(
            zs.at[way, j], zr.at[way, j], zs_sem.at[way, j], zr_sem.at[way, j],
            device_id=(s, (up, down)[way]), device_id_type=MESH,
        )

    def plane_send(src, dst, send_sem, recv_sem, j):
        def one(d):
            pltpu.make_async_remote_copy(
                src.at[j, d], dst.at[j, s], send_sem.at[j], recv_sem.at[j],
                device_id=(d, c), device_id_type=MESH,
            ).start()

        plane_each(one)
        dst[j, s] = src[j, s]

    def plane_wait(src, dst, send_sem, recv_sem, j):
        return pltpu.make_async_remote_copy(
            src.at[j, pl.ds(0, SEQ - 1)], dst.at[j, pl.ds(0, SEQ - 1)],
            send_sem.at[j], recv_sem.at[j], device_id=(s, c), device_id_type=MESH,
        )

    def to_blocks(values, dst, j):
        for a in range(OWN_A):
            part = values[a * N1 : (a + 1) * N1].T.reshape(SEQ, CD, N1)
            bounce[:, a * CD : (a + 1) * CD, :] = part
        dst[j] = bounce[...].astype(BF16)

    def chunk(j):
        return pl.ds(pl.multiple_of(j * CW, CW), CW)

    def project_far(j, carry):
        @pl.when(j > 0)
        def _():
            far_copy(j).wait()

        z2s[j] = jnp.dot(tok[...], wfar[j], preferred_element_type=F32).astype(BF16)

        @pl.when(j == 0)
        def _():
            pl.semaphore_wait(barrier, SEQ + 1)

        z2_copy(j, 0).start()
        z2_copy(j, 1).start()

        @pl.when(j == 0)
        def _():
            loads[3].start()
            for way in range(2):
                near_copy(way, 0).start()

        return carry

    def project_near(j, carry):
        for way in range(2):
            near_copy(way, j).wait()
            part = jnp.dot(tok[...], wnear[way, lax.rem(j, 2)], preferred_element_type=F32)

            @pl.when(j + 2 < NC)
            def _():
                near_copy(way, j + 2).start()

            mine, other = pl.ds(way * HALF, HALF), pl.ds((1 - way) * HALF, HALF)
            z2_copy(j, way).wait_recv()
            zs[way, j, other] = part[(1 - way) * HALF : (2 - way) * HALF].astype(BF16)
            zs[way, j, mine] = (
                part[way * HALF : (way + 1) * HALF] + z2r[j, mine].astype(F32)
            ).astype(BF16)
            z_copy(j, way).start()
        return carry

    def project_own(j, carry):
        own_copy(j).wait()
        own[j] = jnp.dot(tok[...], wown[j], preferred_element_type=F32)
        return carry

    def block_filters(j, carry):
        to_blocks(fl[:, chunk(j)].astype(F32), fs, (0, slice(None), pl.ds(pl.multiple_of(j * BR, BR), BR)))
        return carry

    lax.fori_loop(0, NC, project_far, 0)
    for way in range(2):
        near_copy(way, 1).start()
    for i in (1, 4, 5, 6, 9):
        loads[i].start()
    loads[3].wait()
    lax.fori_loop(0, NC, block_filters, 0)
    plane_send(fs, fr, fs_sem, fr_sem, 0)
    for j in range(NC):
        own_copy(j).start()
    for i in (2, 7, 8):
        loads[i].start()
    lax.fori_loop(0, NC, project_near, 0)
    lax.fori_loop(0, NC, project_own, 0)
    for i in (1, 2, 4, 5, 6, 7, 8, 9):
        loads[i].wait()

    def column(i):
        return pl.ds(i * N1, N1)

    def forward():
        for i in range(CD):
            pos[:, column(i)] = lanes[pl.ds(i, N1, stride=CD), :].astype(BF16)
        first[...] = jnp.dot(fwd[...], pos[...], preferred_element_type=F32)
        for i in range(CD):
            re, im = first[:N1, column(i)], first[N1:, column(i)]
            rows[column(i), :N1] = (re * tw[0] - im * tw[1]).astype(BF16)
            rows[column(i), N1:] = (re * tw[1] + im * tw[0]).astype(BF16)
        return jnp.dot(rows[...], mid[...], preferred_element_type=F32)

    def load_lanes(src, j):
        lanes[...] = src[j].astype(F32).reshape(SEQ * BR, N1)

    def transform_filters(j, carry):
        load_lanes(fr, (0, slice(None), pl.ds(pl.multiple_of(j * BR, BR), BR)))
        spec[j] = forward()
        return carry

    plane_wait(fs, fr, fs_sem, fr_sem, 0).wait_recv()
    transform_filters(0, 0)

    def gather_sums(j):
        z_copy(j, 0).wait_recv()
        z_copy(j, 1).wait_recv()
        value = own[j] + zr[0, j].astype(F32) + zr[1, j].astype(F32)
        mix = (gk[:, chunk(j)].astype(F32) * value).astype(BF16)
        mixed[:, chunk(j)] = mix
        to_blocks(mix.astype(F32), xs, j)
        plane_send(xs, xr, xs_sem, xr_sem, j)

    def convolve(j):
        plane_wait(xs, xr, xs_sem, xr_sem, j).wait_recv()
        load_lanes(xr, j)
        second[...] = forward()
        for i in range(CD):
            re, im = second[column(i), :N1], second[column(i), N1:]
            fre, fim = spec[j, column(i), :N1], spec[j, column(i), N1:]
            rows[column(i), :N1] = (re * fre - im * fim).astype(BF16)
            rows[column(i), N1:] = (re * fim + im * fre).astype(BF16)
        second[...] = jnp.dot(rows[...], midi[...], preferred_element_type=F32)
        for i in range(CD):
            re, im = second[column(i), :N1], second[column(i), N1:]
            back[:N1, column(i)] = (re * tw[0] + im * tw[1]).astype(BF16)
            back[N1:, column(i)] = (im * tw[0] - re * tw[1]).astype(BF16)
        conv = jnp.dot(inv[...], back[...], preferred_element_type=F32)
        for i in range(CD):
            turns[pl.ds(i, N1, stride=CD), :] = conv[:, i * N1 : (i + 1) * N1]
        ys[j] = turns[...].reshape(SEQ, BR, N1).astype(BF16)
        plane_send(ys, yr, ys_sem, yr_sem, j)

    def out_copy(j):
        return pltpu.make_async_copy(out.at[:, chunk(j)], out_hbm.at[:, chunk(j)], out_sem.at[j])

    def finalize(j):
        plane_wait(ys, yr, ys_sem, yr_sem, j).wait_recv()
        bounce[...] = yr[j].astype(F32)
        for a in range(OWN_A):
            conv = bounce[:, a * CD : (a + 1) * CD, :].reshape(CW, N1).T
            own_rows = pl.ds(a * N1, N1)
            total = conv + skip[:, chunk(j)] * mixed[own_rows, chunk(j)].astype(F32)
            out[own_rows, chunk(j)] = (gq[own_rows, chunk(j)].astype(F32) * total).astype(BF16)
        out_copy(j).start()

    def pipeline(j, carry):
        gather_sums(j)

        @pl.when(j == 0)
        def _():
            lax.fori_loop(1, NC, transform_filters, 0)

        @pl.when(j >= 1)
        def _():
            convolve(j - 1)

        return carry

    def finish(j, carry):
        finalize(j)
        return carry

    lax.fori_loop(0, NC, pipeline, 0)
    lax.fori_loop(0, NC - 2, finish, 0)
    convolve(NC - 1)
    lax.fori_loop(NC - 2, NC, finish, 0)

    def drain(j, carry):
        out_copy(j).wait()
        for way in range(2):
            z2_copy(j, way).wait_send()
            z_copy(j, way).wait_send()
        plane_wait(xs, xr, xs_sem, xr_sem, j).wait_send()
        plane_wait(ys, yr, ys_sem, yr_sem, j).wait_send()
        return carry

    plane_wait(fs, fr, fs_sem, fr_sem, 0).wait_send()
    lax.fori_loop(0, NC, drain, 0)


def local(tokens, w_in, gate_k, gate_q, filters, skip):
    any_spec = pl.BlockSpec(memory_space=pl.ANY)
    vm = pltpu.VMEM
    dma = pltpu.SemaphoreType.DMA
    block = (NC, SEQ, BR, N1)
    scratch = [
        vm((ROWS, FEAT), BF16), vm((NC, FEAT, CW), BF16), vm((2, 2, FEAT, CW), BF16), vm((NC, FEAT, CW), BF16),
        vm((ROWS, WIDTH), BF16), vm((ROWS, WIDTH), BF16), vm((ROWS, WIDTH), BF16), vm((1, WIDTH), F32),
        vm((2 * N1, N1), BF16), vm((2 * N1, 2 * N1), BF16), vm((2 * N1, 2 * N1), BF16),
        vm((N1, 2 * N1), BF16), vm((2, N1, N1), F32),
        vm((NC, ROWS, CW), BF16), vm((NC, ROWS, CW), BF16),
        vm((2, NC, ROWS, CW), BF16), vm((2, NC, ROWS, CW), BF16), vm((NC, ROWS, CW), F32),
        vm((ROWS, WIDTH), BF16), vm((ROWS, WIDTH), BF16),
        vm((1, SEQ, NC * BR, N1), BF16), vm((1, SEQ, NC * BR, N1), BF16),
        vm(block, BF16), vm(block, BF16), vm(block, BF16), vm(block, BF16),
        vm((SEQ, BR, N1), F32), vm((SEQ * BR, N1), F32), vm((SEQ * BR, N1), F32), vm((NC, CD * N1, 2 * N1), F32),
        vm((N1, CD * N1), BF16), vm((2 * N1, CD * N1), F32), vm((CD * N1, 2 * N1), BF16),
        vm((CD * N1, 2 * N1), F32), vm((2 * N1, CD * N1), BF16),
        dma((10,)), dma((NC,)), dma((2, 2)), dma((NC,)), dma((NC,)),
        dma((NC, 2)), dma((NC, 2)), dma((2, NC)), dma((2, NC)),
        dma((1,)), dma((1,)), dma((NC,)), dma((NC,)), dma((NC,)), dma((NC,)),
    ]
    return pl.pallas_call(
        kernel,
        out_shape=jax.ShapeDtypeStruct((ROWS, WIDTH), BF16),
        in_specs=[any_spec] * 11,
        out_specs=any_spec,
        scratch_shapes=scratch,
        compiler_params=pltpu.CompilerParams(
            collective_id=0, has_side_effects=True, vmem_limit_bytes=60 * 2**20
        ),
        name="hyena_block",
    )(tokens, w_in, gate_k, gate_q, filters, skip.reshape(1, WIDTH), *tables())


def solution(mesh):
    in_specs = (
        P("seq", "chan"),
        P("chan", None),
        P("seq", "chan"),
        P("seq", "chan"),
        P("seq", "chan"),
        P("chan"),
    )
    out_specs = P("seq", "chan")
    return jax.shard_map(local, mesh=mesh, in_specs=in_specs, out_specs=out_specs, check_vma=False)
```

```python
import math

import jax
import jax.numpy as jnp
import numpy as np
from jax import lax
from jax.experimental import pallas as pl
from jax.experimental.pallas import tpu as pltpu
from jax.sharding import PartitionSpec as P

MESH = pl.DeviceIdType.MESH
SEQ = 32
CHAN = 4
ROWS = 512
FEAT = 2048
WIDTH = 1024
N1 = 128
OWN_A = ROWS // N1
CHIPS = SEQ // 2
NC = 4
CW = WIDTH // NC
CD = CW // SEQ
BR = OWN_A * CD
HALF = ROWS // 2
HW = CW // 2
LAST = NC - 1
F32, BF16 = jnp.float32, jnp.bfloat16


def tables():
    n = N1 * N1
    k = np.arange(N1, dtype=np.float64)
    first = 2.0 * math.pi / N1 * np.outer(k + 0.25, k)
    fwd = np.concatenate([np.cos(first), -np.sin(first)], 0)
    inv = fwd.T / n
    turn = 2.0 * math.pi / n * np.outer(k + 0.25, k)
    tw = np.stack([np.cos(turn), -np.sin(turn)])
    second = 2.0 * math.pi / N1 * np.outer(k, k)
    c, s = np.cos(second), np.sin(second)
    mid = np.block([[c, -s], [s, c]])
    mid_inv = np.block([[c, s], [-s, c]])
    bf = [jnp.asarray(m, F32).astype(BF16) for m in (fwd, mid, mid_inv, inv)]
    return (*bf, jnp.asarray(tw, F32))


def kernel(
    tok_hbm, w_hbm, gk_hbm, gq_hbm, fl_hbm, skip_hbm, fwd_hbm, mid_hbm, midi_hbm, inv_hbm, tw_hbm,
    out,
    tok, wfar, wnear, wown, gk, gq, fl, skip, fwd, mid, midi, inv, tw,
    z2s, z2r, zs, zr, own, mixed,
    fs, fr, xs, xr, ys, yr, bounce, lanes, turns, spec, pos, first, rows, second, back,
    line_sem, tok_sem, in_sem, wfar_sem, wnear_sem, wown_sem,
    z2s_sem, z2r_sem, zs_sem, zr_sem, fs_sem, fr_sem, xs_sem, xr_sem, ys_sem, yr_sem,
):
    s, c = lax.axis_index("seq"), lax.axis_index("chan")
    up, down, far = lax.rem(c + 1, CHAN), lax.rem(c + 3, CHAN), lax.rem(c + 2, CHAN)
    ex, why, core = s // 8, lax.rem(s // 2, 4), lax.rem(s, 2)

    me = core * CHIPS + s // 2

    def plane_half(body, h):
        def step(m, carry):
            q = lax.rem(11 * m, CHIPS)
            chip = lax.rem(ex + q // 4, 4) * 4 + lax.rem(why + lax.rem(q, 4), 4)
            body(chip * 2 + h, h * CHIPS + chip)
            return carry

        lax.fori_loop(1, CHIPS, step, 0)

    def plane_each(body):
        def step(m, carry):
            q = lax.rem(11 * m, CHIPS)
            chip = lax.rem(ex + q // 4, 4) * 4 + lax.rem(why + lax.rem(q, 4), 4)
            body(chip * 2 + core, core * CHIPS + chip)
            body(chip * 2 + 1 - core, (1 - core) * CHIPS + chip)
            return carry

        lax.fori_loop(1, CHIPS, step, 0)
        body(s + 1 - 2 * core, (1 - core) * CHIPS + s // 2)

    tok_loads = [
        pltpu.make_async_copy(tok_hbm.at[pl.ds(h * HALF, HALF)], tok.at[pl.ds(h * HALF, HALF)], tok_sem.at[h])
        for h in range(2)
    ]
    loads = [
        pltpu.make_async_copy(a, b, in_sem.at[i])
        for i, (a, b) in enumerate(
            [(gk_hbm, gk), (gq_hbm, gq), (fl_hbm, fl), (skip_hbm, skip), (fwd_hbm, fwd),
             (mid_hbm, mid), (midi_hbm, midi), (inv_hbm, inv), (tw_hbm, tw)]
        )
    ]

    def w_copy(owner, j, dst, sem):
        col = pl.multiple_of(owner * WIDTH + j * CW, CW)
        return pltpu.make_async_copy(w_hbm.at[:, pl.ds(col, CW)], dst, sem)

    def far_copy(j):
        return w_copy(far, j, wfar.at[j], wfar_sem.at[j])

    def near_copy(way, j):
        slot = lax.rem(j, 2)
        return w_copy((up, down)[way], j, wnear.at[way, slot], wnear_sem.at[way, slot])

    def own_copy(j):
        return w_copy(c, j, wown.at[j], wown_sem.at[j])

    tok_loads[0].start()
    far_copy(0).start()

    barrier = pltpu.get_barrier_semaphore()
    line = [lax.rem(ex + k, 4) * 8 + lax.rem(s, 8) for k in range(1, 4)]
    for z in (up, down):
        pl.semaphore_signal(barrier, inc=1, device_id=(s, z), device_id_type=MESH)
    for d in line + [ex * 8 + lax.rem(s + k, 8) for k in range(1, 8)]:
        pl.semaphore_signal(barrier, inc=1, device_id=(d, c), device_id_type=MESH)

    def z2_copy(j, half):
        half_rows = pl.ds(half * HALF, HALF)
        return pltpu.make_async_remote_copy(
            z2s.at[j, half_rows], z2r.at[j, half_rows], z2s_sem.at[j, half], z2r_sem.at[j, half],
            device_id=(s, (up, down)[half]), device_id_type=MESH,
        )

    def z_copy(j, way):
        return pltpu.make_async_remote_copy(
            zs.at[way, j], zr.at[way, j], zs_sem.at[way, j], zr_sem.at[way, j],
            device_id=(s, (up, down)[way]), device_id_type=MESH,
        )

    def z_last(h, way):
        cols = pl.ds(pl.multiple_of(h * HW, HW), HW)
        return pltpu.make_async_remote_copy(
            zs.at[way, LAST, :, cols], zr.at[way, LAST, :, cols],
            zs_sem.at[way, LAST + h], zr_sem.at[way, LAST + h],
            device_id=(s, (up, down)[way]), device_id_type=MESH,
        )

    def block_send(src, dst, send_sem, recv_sem, d):
        pltpu.make_async_remote_copy(
            src, dst, send_sem, recv_sem, device_id=(d, c), device_id_type=MESH
        ).start()

    def send_filters():
        plane_each(
            lambda d, slot: block_send(fs.at[slot], fr.at[s], fs_sem.at[0], fr_sem.at[0], d)
        )
        fr[s] = fs[me]

    def send_mixed(j, h):
        def one(d, slot):
            block_send(xs.at[j, slot], xr.at[j, s], xs_sem.at[j], xr_sem.at[j], d)

        plane_half(one, h)

        @pl.when(core == h)
        def _():
            xr[j, s] = xs[j, me]

        @pl.when(core != h)
        def _():
            one(s + 1 - 2 * core, h * CHIPS + s // 2)

    def send_conv(j):
        plane_each(
            lambda d, slot: block_send(
                ys.at[j, d], yr.at[j, me], ys_sem.at[j], yr_sem.at[j, core], d
            )
        )
        yr[j, me] = ys[j, s]

    def block_wait(buf, send_sem, recv_sem, count):
        part = buf.at[pl.ds(0, count)]
        return pltpu.make_async_remote_copy(
            part, part, send_sem, recv_sem, device_id=(s, c), device_id_type=MESH
        )

    def to_blocks(values, h):
        for a in range(OWN_A):
            part = values[a * N1 : (a + 1) * N1].T.reshape(CHIPS, CD, N1)
            bounce[h, :, a * CD : (a + 1) * CD, :] = part
        return bounce[h].astype(BF16)

    def half(j, h):
        return pl.ds(pl.multiple_of(j * CW + h * HW, HW), HW)

    def by_core(h):
        return pl.ds(h * CHIPS, CHIPS)

    def project_far(j, carry):
        far_copy(j).wait()
        z2s[j] = jnp.dot(tok[...], wfar[j], preferred_element_type=F32).astype(BF16)

        @pl.when(j < LAST)
        def _():
            z2_copy(j, 0).start()
            z2_copy(j, 1).start()

        return carry

    def project_near(j, carry):
        for way in range(2):
            near_copy(way, j).wait()
            part = jnp.dot(tok[...], wnear[way, lax.rem(j, 2)], preferred_element_type=F32)

            @pl.when(j + 2 < NC)
            def _():
                near_copy(way, j + 2).start()

            mine, other = pl.ds(way * HALF, HALF), pl.ds((1 - way) * HALF, HALF)
            z2_copy(j, way).wait_recv()
            zs[way, j, other] = part[(1 - way) * HALF : (2 - way) * HALF].astype(BF16)
            zs[way, j, mine] = (
                part[way * HALF : (way + 1) * HALF] + z2r[j, mine].astype(F32)
            ).astype(BF16)

            @pl.when(j == 0)
            def _():
                z_copy(0, way).start()

        return carry

    def start_sums(copy, j):
        for way in range(2):
            copy(j, way).start()

    def project_own(j, carry):
        own_copy(j).wait()
        own[j] = jnp.dot(tok[...], wown[j], preferred_element_type=F32)
        return carry

    def block_filters(j, carry):
        rows_of = pl.ds(pl.multiple_of(j * BR, BR), BR)
        for h in range(2):
            fs[by_core(h), rows_of] = to_blocks(fl[:, half(j, h)].astype(F32), h)
        return carry

    tok_loads[0].wait()
    far_copy(0).wait()
    tok_loads[1].start()
    for j in range(1, NC):
        far_copy(j).start()
    for h in range(2):
        if h:
            tok_loads[1].wait()
        top = pl.ds(h * HALF, HALF)
        z2s[0, top] = jnp.dot(tok[top], wfar[0], preferred_element_type=F32).astype(BF16)
        if not h:
            pl.semaphore_wait(barrier, 12)
        z2_copy(0, h).start()
        if not h:
            for d in line:
                pl.semaphore_signal(line_sem, inc=1, device_id=(d, c), device_id_type=MESH)
    loads[2].start()
    for way in range(2):
        near_copy(way, 0).start()
    lax.fori_loop(1, 2, project_far, 0)
    for way in range(2):
        near_copy(way, 1).start()
    for i in (0, 3, 4, 5, 8):
        loads[i].start()
    loads[2].wait()
    lax.fori_loop(0, NC, block_filters, 0)
    pl.semaphore_wait(line_sem, 3)
    send_filters()
    for j in range(NC):
        own_copy(j).start()
    for i in (1, 6, 7):
        loads[i].start()
    lax.fori_loop(0, 2, project_near, 0)
    lax.fori_loop(2, 3, project_far, 0)
    lax.fori_loop(0, NC, project_own, 0)
    start_sums(z_copy, 1)
    lax.fori_loop(LAST, NC, project_far, 0)
    for i in (0, 1, 3, 4, 5, 6, 7, 8):
        loads[i].wait()

    def column(i):
        return pl.ds(i * N1, N1)

    def forward():
        for i in range(CD):
            pos[:, column(i)] = lanes[pl.ds(i, N1, stride=CD), :].astype(BF16)
        first[...] = jnp.dot(fwd[...], pos[...], preferred_element_type=F32)
        for i in range(CD):
            re, im = first[:N1, column(i)], first[N1:, column(i)]
            rows[column(i), :N1] = (re * tw[0] - im * tw[1]).astype(BF16)
            rows[column(i), N1:] = (re * tw[1] + im * tw[0]).astype(BF16)
        return jnp.dot(rows[...], mid[...], preferred_element_type=F32)

    def load_lanes(src, j):
        lanes[...] = src[j].astype(F32).reshape(SEQ * BR, N1)

    def transform_filters(j, carry):
        load_lanes(fr, (slice(None), pl.ds(pl.multiple_of(j * BR, BR), BR)))
        spec[j] = forward()
        return carry


    def gather_sums(j, h):
        cols = slice(h * HW, (h + 1) * HW)
        value = own[j, :, cols] + zr[0, j, :, cols].astype(F32) + zr[1, j, :, cols].astype(F32)
        mix = (gk[:, half(j, h)].astype(F32) * value).astype(BF16)
        mixed[:, half(j, h)] = mix
        xs[j, by_core(h)] = to_blocks(mix.astype(F32), h)
        send_mixed(j, h)

    def convolve(j):
        block_wait(xr.at[j], xs_sem.at[j], xr_sem.at[j], SEQ - 1).wait_recv()
        load_lanes(xr, j)
        second[...] = forward()
        for i in range(CD):
            re, im = second[column(i), :N1], second[column(i), N1:]
            fre, fim = spec[j, column(i), :N1], spec[j, column(i), N1:]
            rows[column(i), :N1] = (re * fre - im * fim).astype(BF16)
            rows[column(i), N1:] = (re * fim + im * fre).astype(BF16)
        second[...] = jnp.dot(rows[...], midi[...], preferred_element_type=F32)
        for i in range(CD):
            re, im = second[column(i), :N1], second[column(i), N1:]
            back[:N1, column(i)] = (re * tw[0] + im * tw[1]).astype(BF16)
            back[N1:, column(i)] = (im * tw[0] - re * tw[1]).astype(BF16)
        conv = jnp.dot(inv[...], back[...], preferred_element_type=F32)
        for i in range(CD):
            turns[pl.ds(i, N1, stride=CD), :] = conv[:, i * N1 : (i + 1) * N1]
        ys[j] = turns[...].reshape(SEQ, BR, N1).astype(BF16)
        send_conv(j)

    def finalize(j, h):
        @pl.when(core == h)
        def _():
            block_wait(yr.at[j], ys_sem.at[j], yr_sem.at[j, h], CHIPS - 1).wait_recv()

        @pl.when(core != h)
        def _():
            block_wait(yr.at[j], ys_sem.at[j], yr_sem.at[j, h], CHIPS).wait_recv()

        bounce[h] = yr[j, by_core(h)].astype(F32)
        for a in range(OWN_A):
            conv = bounce[h, :, a * CD : (a + 1) * CD, :].reshape(HW, N1).T
            here = pl.ds(a * N1, N1)
            total = conv + skip[:, half(j, h)] * mixed[here, half(j, h)].astype(F32)
            out[here, half(j, h)] = (gq[here, half(j, h)].astype(F32) * total).astype(BF16)

    def gather_chunk(j):
        z_copy(j, 0).wait_recv()
        z_copy(j, 1).wait_recv()
        gather_sums(j, 0)
        gather_sums(j, 1)

    def finish(j, carry):
        finalize(j, 0)
        finalize(j, 1)
        return carry

    def gather_last(h):
        z_last(h, 0).wait_recv()
        z_last(h, 1).wait_recv()
        gather_sums(LAST, h)

    gather_chunk(0)
    start_sums(z2_copy, LAST)
    lax.fori_loop(2, 3, project_near, 0)
    start_sums(z_copy, 2)
    block_wait(fr, fs_sem.at[0], fr_sem.at[0], SEQ - 1).wait_recv()
    lax.fori_loop(0, NC, transform_filters, 0)
    convolve(0)
    gather_chunk(1)
    lax.fori_loop(3, 4, project_near, 0)
    start_sums(z_last, 0)
    gather_chunk(2)
    start_sums(z_last, 1)
    convolve(1)
    gather_last(0)
    gather_last(1)
    convolve(2)
    lax.fori_loop(0, 2, finish, 0)
    convolve(3)
    lax.fori_loop(2, 4, finish, 0)

    def drain(j, carry):
        for h in range(2):
            z2_copy(j, h).wait_send()

            @pl.when(j < LAST)
            def _():
                z_copy(j, h).wait_send()

        block_wait(xr.at[j], xs_sem.at[j], xr_sem.at[j], SEQ - 1).wait_send()
        block_wait(yr.at[j], ys_sem.at[j], yr_sem.at[j, 0], SEQ - 1).wait_send()
        return carry

    for h in range(2):
        for way in range(2):
            z_last(h, way).wait_send()
    block_wait(fr, fs_sem.at[0], fr_sem.at[0], SEQ - 1).wait_send()
    lax.fori_loop(0, NC, drain, 0)


def local(tokens, w_in, gate_k, gate_q, filters, skip):
    any_spec = pl.BlockSpec(memory_space=pl.ANY)
    vm = pltpu.VMEM
    dma = pltpu.SemaphoreType.DMA
    block = (NC, SEQ, BR, N1)
    scratch = [
        vm((ROWS, FEAT), BF16), vm((NC, FEAT, CW), BF16), vm((2, 2, FEAT, CW), BF16), vm((NC, FEAT, CW), BF16),
        vm((ROWS, WIDTH), BF16), vm((ROWS, WIDTH), BF16), vm((ROWS, WIDTH), BF16), vm((1, WIDTH), F32),
        vm((2 * N1, N1), BF16), vm((2 * N1, 2 * N1), BF16), vm((2 * N1, 2 * N1), BF16),
        vm((N1, 2 * N1), BF16), vm((2, N1, N1), F32),
        vm((NC, ROWS, CW), BF16), vm((NC, ROWS, CW), BF16),
        vm((2, NC, ROWS, CW), BF16), vm((2, NC, ROWS, CW), BF16), vm((NC, ROWS, CW), F32),
        vm((ROWS, WIDTH), BF16),
        vm((SEQ, NC * BR, N1), BF16), vm((SEQ, NC * BR, N1), BF16),
        vm(block, BF16), vm(block, BF16), vm(block, BF16), vm(block, BF16),
        vm((2, CHIPS, BR, N1), F32), vm((SEQ * BR, N1), F32), vm((SEQ * BR, N1), F32), vm((NC, CD * N1, 2 * N1), F32),
        vm((N1, CD * N1), BF16), vm((2 * N1, CD * N1), F32), vm((CD * N1, 2 * N1), BF16),
        vm((CD * N1, 2 * N1), F32), vm((2 * N1, CD * N1), BF16),
        pltpu.SemaphoreType.REGULAR, dma((2,)), dma((9,)), dma((NC,)), dma((2, 2)), dma((NC,)),
        dma((NC, 2)), dma((NC, 2)), dma((2, NC + 1)), dma((2, NC + 1)),
        dma((1,)), dma((1,)), dma((NC,)), dma((NC,)), dma((NC,)), dma((NC, 2)),
    ]
    return pl.pallas_call(
        kernel,
        out_shape=pltpu.VMEM((ROWS, WIDTH), BF16),
        in_specs=[any_spec] * 11,
        out_specs=pl.BlockSpec(memory_space=pltpu.VMEM),
        scratch_shapes=scratch,
        compiler_params=pltpu.CompilerParams(
            collective_id=0, has_side_effects=True, vmem_limit_bytes=56 * 2**20
        ),
        name="hyena_block",
    )(tokens, w_in, gate_k, gate_q, filters, skip.reshape(1, WIDTH), *tables())


def solution(mesh):
    in_specs = (
        P("seq", "chan"),
        P("chan", None),
        P("seq", "chan"),
        P("seq", "chan"),
        P("seq", "chan"),
        P("chan"),
    )
    out_specs = P("seq", "chan")
    return jax.shard_map(local, mesh=mesh, in_specs=in_specs, out_specs=out_specs, check_vma=False)
```

```python
import math

import jax
import jax.numpy as jnp
import numpy as np
from jax import lax
from jax.experimental import pallas as pl
from jax.experimental.pallas import tpu as pltpu
from jax.sharding import PartitionSpec as P

MESH = pl.DeviceIdType.MESH
SEQ = 32
CHAN = 4
ROWS = 512
FEAT = 2048
WIDTH = 1024
N1 = 128
OWN_A = ROWS // N1
CHIPS = SEQ // 2
NC = 4
CW = WIDTH // NC
CD = CW // SEQ
BR = OWN_A * CD
HALF = ROWS // 2
HW = CW // 2
LAST = NC - 1
F32, BF16 = jnp.float32, jnp.bfloat16


def tables():
    n = N1 * N1
    k = np.arange(N1, dtype=np.float64)
    first = 2.0 * math.pi / N1 * np.outer(k + 0.25, k)
    fwd = np.concatenate([np.cos(first), -np.sin(first)], 0)
    inv = fwd.T / n
    turn = 2.0 * math.pi / n * np.outer(k + 0.25, k)
    tw = np.stack([np.cos(turn), -np.sin(turn)])
    second = 2.0 * math.pi / N1 * np.outer(k, k)
    c, s = np.cos(second), np.sin(second)
    mid = np.block([[c, -s], [s, c]])
    mid_inv = np.block([[c, s], [-s, c]])
    bf = [jnp.asarray(m, F32).astype(BF16) for m in (fwd, mid, mid_inv, inv)]
    return (*bf, jnp.asarray(tw, F32))


def kernel(
    tok_hbm, w_hbm, gk_hbm, gq_hbm, fl_hbm, skip_hbm, fwd_hbm, mid_hbm, midi_hbm, inv_hbm, tw_hbm,
    out,
    tok, wfar, wnear, wown, gk, gq, fl, skip, fwd, mid, midi, inv, tw,
    z2s, z2r, zs, zr, own, mixed,
    fs, fr, xs, xr, ys, yr, bounce, lanes, turns, spec, pos, first, rows, second, back,
    line_sem, tok_sem, in_sem, wfar_sem, wnear_sem, wown_sem,
    z2s_sem, z2r_sem, zs_sem, zr_sem, fs_sem, fr_sem, xs_sem, xr_sem, ys_sem, yr_sem,
):
    s, c = lax.axis_index("seq"), lax.axis_index("chan")
    up, down, far = lax.rem(c + 1, CHAN), lax.rem(c + 3, CHAN), lax.rem(c + 2, CHAN)
    ex, why, core = s // 8, lax.rem(s // 2, 4), lax.rem(s, 2)

    me = core * CHIPS + s // 2

    def plane_half(body, h):
        def step(m, carry):
            q = lax.rem(11 * m, CHIPS)
            chip = lax.rem(ex + q // 4, 4) * 4 + lax.rem(why + lax.rem(q, 4), 4)
            body(chip * 2 + h, h * CHIPS + chip)
            return carry

        lax.fori_loop(1, CHIPS, step, 0)

    def plane_each(body):
        def step(m, carry):
            q = lax.rem(11 * m, CHIPS)
            chip = lax.rem(ex + q // 4, 4) * 4 + lax.rem(why + lax.rem(q, 4), 4)
            body(chip * 2 + core, core * CHIPS + chip)
            body(chip * 2 + 1 - core, (1 - core) * CHIPS + chip)
            return carry

        lax.fori_loop(1, CHIPS, step, 0)
        body(s + 1 - 2 * core, (1 - core) * CHIPS + s // 2)

    tok_loads = [
        pltpu.make_async_copy(tok_hbm.at[pl.ds(h * HALF, HALF)], tok.at[pl.ds(h * HALF, HALF)], tok_sem.at[h])
        for h in range(2)
    ]
    loads = [
        pltpu.make_async_copy(a, b, in_sem.at[i])
        for i, (a, b) in enumerate(
            [(gk_hbm, gk), (gq_hbm, gq), (fl_hbm, fl), (skip_hbm, skip), (fwd_hbm, fwd),
             (mid_hbm, mid), (midi_hbm, midi), (inv_hbm, inv), (tw_hbm, tw)]
        )
    ]

    def w_copy(owner, j, dst, sem):
        col = pl.multiple_of(owner * WIDTH + j * CW, CW)
        return pltpu.make_async_copy(w_hbm.at[:, pl.ds(col, CW)], dst, sem)

    def far_copy(j):
        return w_copy(far, j, wfar.at[j], wfar_sem.at[j])

    def near_copy(way, j):
        slot = lax.rem(j, 2)
        return w_copy((up, down)[way], j, wnear.at[way, slot], wnear_sem.at[way, slot])

    def own_copy(j):
        return w_copy(c, j, wown.at[j], wown_sem.at[j])

    tok_loads[0].start()
    far_copy(0).start()

    barrier = pltpu.get_barrier_semaphore()
    line = [lax.rem(ex + k, 4) * 8 + lax.rem(s, 8) for k in range(1, 4)]
    for z in (up, down):
        pl.semaphore_signal(barrier, inc=1, device_id=(s, z), device_id_type=MESH)
    for d in line + [ex * 8 + lax.rem(s + k, 8) for k in range(1, 8)]:
        pl.semaphore_signal(barrier, inc=1, device_id=(d, c), device_id_type=MESH)

    def z2_copy(j, half):
        half_rows = pl.ds(half * HALF, HALF)
        return pltpu.make_async_remote_copy(
            z2s.at[j, half_rows], z2r.at[j, half_rows], z2s_sem.at[j, half], z2r_sem.at[j, half],
            device_id=(s, (up, down)[half]), device_id_type=MESH,
        )

    def z_copy(j, way):
        return pltpu.make_async_remote_copy(
            zs.at[way, j], zr.at[way, j], zs_sem.at[way, j], zr_sem.at[way, j],
            device_id=(s, (up, down)[way]), device_id_type=MESH,
        )

    def z_last(h, way):
        cols = pl.ds(pl.multiple_of(h * HW, HW), HW)
        return pltpu.make_async_remote_copy(
            zs.at[way, LAST, :, cols], zr.at[way, LAST, :, cols],
            zs_sem.at[way, LAST + h], zr_sem.at[way, LAST + h],
            device_id=(s, (up, down)[way]), device_id_type=MESH,
        )

    def block_send(src, dst, send_sem, recv_sem, d):
        pltpu.make_async_remote_copy(
            src, dst, send_sem, recv_sem, device_id=(d, c), device_id_type=MESH
        ).start()

    def send_filters():
        plane_each(
            lambda d, slot: block_send(fs.at[slot], fr.at[s], fs_sem.at[0], fr_sem.at[0], d)
        )
        fr[s] = fs[me]

    def send_mixed(j, h):
        def one(d, slot):
            block_send(xs.at[j, slot], xr.at[j, s], xs_sem.at[j], xr_sem.at[j], d)

        plane_half(one, h)

        @pl.when(core == h)
        def _():
            xr[j, s] = xs[j, me]

        @pl.when(core != h)
        def _():
            one(s + 1 - 2 * core, h * CHIPS + s // 2)

    def send_conv(j):
        plane_each(
            lambda d, slot: block_send(
                ys.at[j, d], yr.at[j, me], ys_sem.at[j], yr_sem.at[j, core], d
            )
        )
        yr[j, me] = ys[j, s]

    def block_wait(buf, send_sem, recv_sem, count):
        part = buf.at[pl.ds(0, count)]
        return pltpu.make_async_remote_copy(
            part, part, send_sem, recv_sem, device_id=(s, c), device_id_type=MESH
        )

    def to_blocks(values, h):
        for a in range(OWN_A):
            part = values[a * N1 : (a + 1) * N1].T.reshape(CHIPS, CD, N1)
            bounce[h, :, a * CD : (a + 1) * CD, :] = part
        return bounce[h].astype(BF16)

    def half(j, h):
        return pl.ds(pl.multiple_of(j * CW + h * HW, HW), HW)

    def by_core(h):
        return pl.ds(h * CHIPS, CHIPS)

    def project_far(j, carry):
        far_copy(j).wait()
        z2s[j] = jnp.dot(tok[...], wfar[j], preferred_element_type=F32).astype(BF16)

        @pl.when(j < LAST)
        def _():
            z2_copy(j, 0).start()
            z2_copy(j, 1).start()

        return carry

    def project_near(j, carry):
        for way in range(2):
            near_copy(way, j).wait()
            part = jnp.dot(tok[...], wnear[way, lax.rem(j, 2)], preferred_element_type=F32)

            @pl.when(j + 2 < NC)
            def _():
                near_copy(way, j + 2).start()

            mine, other = pl.ds(way * HALF, HALF), pl.ds((1 - way) * HALF, HALF)
            z2_copy(j, way).wait_recv()
            zs[way, j, other] = part[(1 - way) * HALF : (2 - way) * HALF].astype(BF16)
            zs[way, j, mine] = (
                part[way * HALF : (way + 1) * HALF] + z2r[j, mine].astype(F32)
            ).astype(BF16)

            @pl.when(j == 0)
            def _():
                z_copy(0, way).start()

        return carry

    def start_sums(copy, j):
        for way in range(2):
            copy(j, way).start()

    def project_own(j, carry):
        own_copy(j).wait()
        own[j] = jnp.dot(tok[...], wown[j], preferred_element_type=F32)
        return carry

    def block_filters(j, carry):
        rows_of = pl.ds(pl.multiple_of(j * BR, BR), BR)
        for h in range(2):
            fs[by_core(h), rows_of] = to_blocks(fl[:, half(j, h)].astype(F32), h)
        return carry

    tok_loads[0].wait()
    far_copy(0).wait()
    tok_loads[1].start()
    far_copy(1).start()
    loads[2].start()
    for h in range(2):
        if h:
            tok_loads[1].wait()
        top = pl.ds(h * HALF, HALF)
        z2s[0, top] = jnp.dot(tok[top], wfar[0], preferred_element_type=F32).astype(BF16)
        if not h:
            pl.semaphore_wait(barrier, 12)
        z2_copy(0, h).start()
        if not h:
            for d in line:
                pl.semaphore_signal(line_sem, inc=1, device_id=(d, c), device_id_type=MESH)
    for way in range(2):
        near_copy(way, 0).start()
    for j in range(2, NC):
        far_copy(j).start()
    lax.fori_loop(1, 2, project_far, 0)
    for way in range(2):
        near_copy(way, 1).start()
    for i in (0, 3, 4, 5, 8):
        loads[i].start()
    loads[2].wait()
    lax.fori_loop(0, NC, block_filters, 0)
    pl.semaphore_wait(line_sem, 3)
    send_filters()
    for j in range(NC):
        own_copy(j).start()
    for i in (1, 6, 7):
        loads[i].start()
    lax.fori_loop(0, 2, project_near, 0)
    lax.fori_loop(2, 3, project_far, 0)
    lax.fori_loop(0, NC, project_own, 0)
    start_sums(z_copy, 1)
    lax.fori_loop(LAST, NC, project_far, 0)
    for i in (0, 1, 3, 4, 5, 6, 7, 8):
        loads[i].wait()

    def column(i):
        return pl.ds(i * N1, N1)

    def forward():
        for i in range(CD):
            pos[:, column(i)] = lanes[pl.ds(i, N1, stride=CD), :].astype(BF16)
        first[...] = jnp.dot(fwd[...], pos[...], preferred_element_type=F32)
        for i in range(CD):
            re, im = first[:N1, column(i)], first[N1:, column(i)]
            rows[column(i), :N1] = (re * tw[0] - im * tw[1]).astype(BF16)
            rows[column(i), N1:] = (re * tw[1] + im * tw[0]).astype(BF16)
        return jnp.dot(rows[...], mid[...], preferred_element_type=F32)

    def load_lanes(src, j):
        lanes[...] = src[j].astype(F32).reshape(SEQ * BR, N1)

    def transform_filters(j, carry):
        load_lanes(fr, (slice(None), pl.ds(pl.multiple_of(j * BR, BR), BR)))
        spec[j] = forward()
        return carry


    def gather_sums(j, h):
        cols = slice(h * HW, (h + 1) * HW)
        value = own[j, :, cols] + zr[0, j, :, cols].astype(F32) + zr[1, j, :, cols].astype(F32)
        mix = (gk[:, half(j, h)].astype(F32) * value).astype(BF16)
        mixed[:, half(j, h)] = mix
        xs[j, by_core(h)] = to_blocks(mix.astype(F32), h)
        send_mixed(j, h)

    def convolve(j):
        block_wait(xr.at[j], xs_sem.at[j], xr_sem.at[j], SEQ - 1).wait_recv()
        load_lanes(xr, j)
        second[...] = forward()
        for i in range(CD):
            re, im = second[column(i), :N1], second[column(i), N1:]
            fre, fim = spec[j, column(i), :N1], spec[j, column(i), N1:]
            rows[column(i), :N1] = (re * fre - im * fim).astype(BF16)
            rows[column(i), N1:] = (re * fim + im * fre).astype(BF16)
        second[...] = jnp.dot(rows[...], midi[...], preferred_element_type=F32)
        for i in range(CD):
            re, im = second[column(i), :N1], second[column(i), N1:]
            back[:N1, column(i)] = (re * tw[0] + im * tw[1]).astype(BF16)
            back[N1:, column(i)] = (im * tw[0] - re * tw[1]).astype(BF16)
        conv = jnp.dot(inv[...], back[...], preferred_element_type=F32)
        for i in range(CD):
            turns[pl.ds(i, N1, stride=CD), :] = conv[:, i * N1 : (i + 1) * N1]
        ys[j] = turns[...].reshape(SEQ, BR, N1).astype(BF16)
        send_conv(j)

    def finalize(j, h):
        @pl.when(core == h)
        def _():
            block_wait(yr.at[j], ys_sem.at[j], yr_sem.at[j, h], CHIPS - 1).wait_recv()

        @pl.when(core != h)
        def _():
            block_wait(yr.at[j], ys_sem.at[j], yr_sem.at[j, h], CHIPS).wait_recv()

        bounce[h] = yr[j, by_core(h)].astype(F32)
        for a in range(OWN_A):
            conv = bounce[h, :, a * CD : (a + 1) * CD, :].reshape(HW, N1).T
            here = pl.ds(a * N1, N1)
            total = conv + skip[:, half(j, h)] * mixed[here, half(j, h)].astype(F32)
            out[here, half(j, h)] = (gq[here, half(j, h)].astype(F32) * total).astype(BF16)

    def gather_chunk(j):
        z_copy(j, 0).wait_recv()
        z_copy(j, 1).wait_recv()
        gather_sums(j, 0)
        gather_sums(j, 1)

    def finish(j, carry):
        finalize(j, 0)
        finalize(j, 1)
        return carry

    def gather_last(h):
        z_last(h, 0).wait_recv()
        z_last(h, 1).wait_recv()
        gather_sums(LAST, h)

    gather_chunk(0)
    start_sums(z2_copy, LAST)
    lax.fori_loop(2, 3, project_near, 0)
    start_sums(z_copy, 2)
    block_wait(fr, fs_sem.at[0], fr_sem.at[0], SEQ - 1).wait_recv()
    lax.fori_loop(0, NC, transform_filters, 0)
    convolve(0)
    gather_chunk(1)
    lax.fori_loop(3, 4, project_near, 0)
    start_sums(z_last, 0)
    gather_chunk(2)
    start_sums(z_last, 1)
    convolve(1)
    gather_last(0)
    gather_last(1)
    convolve(2)
    lax.fori_loop(0, 2, finish, 0)
    convolve(3)
    lax.fori_loop(2, 4, finish, 0)

    def drain(j, carry):
        for h in range(2):
            z2_copy(j, h).wait_send()

            @pl.when(j < LAST)
            def _():
                z_copy(j, h).wait_send()

        block_wait(xr.at[j], xs_sem.at[j], xr_sem.at[j], SEQ - 1).wait_send()
        block_wait(yr.at[j], ys_sem.at[j], yr_sem.at[j, 0], SEQ - 1).wait_send()
        return carry

    for h in range(2):
        for way in range(2):
            z_last(h, way).wait_send()
    block_wait(fr, fs_sem.at[0], fr_sem.at[0], SEQ - 1).wait_send()
    lax.fori_loop(0, NC, drain, 0)


def local(tokens, w_in, gate_k, gate_q, filters, skip):
    any_spec = pl.BlockSpec(memory_space=pl.ANY)
    vm = pltpu.VMEM
    dma = pltpu.SemaphoreType.DMA
    block = (NC, SEQ, BR, N1)
    scratch = [
        vm((ROWS, FEAT), BF16), vm((NC, FEAT, CW), BF16), vm((2, 2, FEAT, CW), BF16), vm((NC, FEAT, CW), BF16),
        vm((ROWS, WIDTH), BF16), vm((ROWS, WIDTH), BF16), vm((ROWS, WIDTH), BF16), vm((1, WIDTH), F32),
        vm((2 * N1, N1), BF16), vm((2 * N1, 2 * N1), BF16), vm((2 * N1, 2 * N1), BF16),
        vm((N1, 2 * N1), BF16), vm((2, N1, N1), F32),
        vm((NC, ROWS, CW), BF16), vm((NC, ROWS, CW), BF16),
        vm((2, NC, ROWS, CW), BF16), vm((2, NC, ROWS, CW), BF16), vm((NC, ROWS, CW), F32),
        vm((ROWS, WIDTH), BF16),
        vm((SEQ, NC * BR, N1), BF16), vm((SEQ, NC * BR, N1), BF16),
        vm(block, BF16), vm(block, BF16), vm(block, BF16), vm(block, BF16),
        vm((2, CHIPS, BR, N1), F32), vm((SEQ * BR, N1), F32), vm((SEQ * BR, N1), F32), vm((NC, CD * N1, 2 * N1), F32),
        vm((N1, CD * N1), BF16), vm((2 * N1, CD * N1), F32), vm((CD * N1, 2 * N1), BF16),
        vm((CD * N1, 2 * N1), F32), vm((2 * N1, CD * N1), BF16),
        pltpu.SemaphoreType.REGULAR, dma((2,)), dma((9,)), dma((NC,)), dma((2, 2)), dma((NC,)),
        dma((NC, 2)), dma((NC, 2)), dma((2, NC + 1)), dma((2, NC + 1)),
        dma((1,)), dma((1,)), dma((NC,)), dma((NC,)), dma((NC,)), dma((NC, 2)),
    ]
    return pl.pallas_call(
        kernel,
        out_shape=pltpu.VMEM((ROWS, WIDTH), BF16),
        in_specs=[any_spec] * 11,
        out_specs=pl.BlockSpec(memory_space=pltpu.VMEM),
        scratch_shapes=scratch,
        compiler_params=pltpu.CompilerParams(
            collective_id=0, has_side_effects=True, vmem_limit_bytes=56 * 2**20
        ),
        name="hyena_block",
    )(tokens, w_in, gate_k, gate_q, filters, skip.reshape(1, WIDTH), *tables())


def solution(mesh):
    in_specs = (
        P("seq", "chan"),
        P("chan", None),
        P("seq", "chan"),
        P("seq", "chan"),
        P("seq", "chan"),
        P("chan"),
    )
    out_specs = P("seq", "chan")
    return jax.shard_map(local, mesh=mesh, in_specs=in_specs, out_specs=out_specs, check_vma=False)
```

```python
import math

import jax
import jax.numpy as jnp
import numpy as np
from jax import lax
from jax.experimental import pallas as pl
from jax.experimental.pallas import tpu as pltpu
from jax.sharding import PartitionSpec as P

MESH = pl.DeviceIdType.MESH
SEQ = 32
CHAN = 4
ROWS = 512
FEAT = 2048
WIDTH = 1024
N1 = 128
OWN_A = ROWS // N1
CHIPS = SEQ // 2
FAR_FIRST = sorted(
    [(q // 4, q % 4) for q in range(1, CHIPS)], key=lambda o: -min(o[0], 4 - o[0]) - min(o[1], 4 - o[1])
)
NC = 4
CW = WIDTH // NC
CD = CW // SEQ
BR = OWN_A * CD
HALF = ROWS // 2
HW = CW // 2
LAST = NC - 1
F32, BF16 = jnp.float32, jnp.bfloat16


def tables():
    n = N1 * N1
    k = np.arange(N1, dtype=np.float64)
    first = 2.0 * math.pi / N1 * np.outer(k + 0.25, k)
    fwd = np.concatenate([np.cos(first), -np.sin(first)], 0)
    inv = fwd.T / n
    turn = 2.0 * math.pi / n * np.outer(k + 0.25, k)
    tw = np.stack([np.cos(turn), -np.sin(turn)])
    second = 2.0 * math.pi / N1 * np.outer(k, k)
    c, s = np.cos(second), np.sin(second)
    mid = np.block([[c, -s], [s, c]])
    mid_inv = np.block([[c, s], [-s, c]])
    bf = [jnp.asarray(m, F32).astype(BF16) for m in (fwd, mid, mid_inv, inv)]
    return (*bf, jnp.asarray(tw, F32))


def kernel(
    tok_hbm, w_hbm, gk_hbm, gq_hbm, fl_hbm, skip_hbm, fwd_hbm, mid_hbm, midi_hbm, inv_hbm, tw_hbm,
    out,
    tok, wfar, wnear, wown, gk, gq, fl, skip, fwd, mid, midi, inv, tw,
    z2s, z2r, zs, zr, own, mixed,
    fs, fr, xs, xr, ys, yr, bounce, lanes, turns, spec, pos, first, rows, second, back,
    line_sem, tok_sem, in_sem, wfar_sem, wnear_sem, wown_sem,
    z2s_sem, z2r_sem, zs_sem, zr_sem, fs_sem, fr_sem, xs_sem, xr_sem, ys_sem, yr_sem,
):
    s, c = lax.axis_index("seq"), lax.axis_index("chan")
    up, down, far = lax.rem(c + 1, CHAN), lax.rem(c + 3, CHAN), lax.rem(c + 2, CHAN)
    ex, why, core = s // 8, lax.rem(s // 2, 4), lax.rem(s, 2)

    me = core * CHIPS + s // 2

    def plane_half(body, h):
        for dx, dy in FAR_FIRST:
            chip = lax.rem(ex + dx, 4) * 4 + lax.rem(why + dy, 4)
            body(chip * 2 + h, h * CHIPS + chip)


    def plane_each(body):
        for dx, dy in FAR_FIRST:
            chip = lax.rem(ex + dx, 4) * 4 + lax.rem(why + dy, 4)
            body(chip * 2 + core, core * CHIPS + chip)
            body(chip * 2 + 1 - core, (1 - core) * CHIPS + chip)

        body(s + 1 - 2 * core, (1 - core) * CHIPS + s // 2)

    tok_loads = [
        pltpu.make_async_copy(tok_hbm.at[pl.ds(h * HALF, HALF)], tok.at[pl.ds(h * HALF, HALF)], tok_sem.at[h])
        for h in range(2)
    ]
    loads = [
        pltpu.make_async_copy(a, b, in_sem.at[i])
        for i, (a, b) in enumerate(
            [(gk_hbm, gk), (gq_hbm, gq), (fl_hbm, fl), (skip_hbm, skip), (fwd_hbm, fwd),
             (mid_hbm, mid), (midi_hbm, midi), (inv_hbm, inv), (tw_hbm, tw)]
        )
    ]

    def w_copy(owner, j, dst, sem):
        col = pl.multiple_of(owner * WIDTH + j * CW, CW)
        return pltpu.make_async_copy(w_hbm.at[:, pl.ds(col, CW)], dst, sem)

    def far_copy(j):
        return w_copy(far, j, wfar.at[j], wfar_sem.at[j])

    def near_copy(way, j):
        slot = lax.rem(j, 2)
        return w_copy((up, down)[way], j, wnear.at[way, slot], wnear_sem.at[way, slot])

    def own_copy(j):
        return w_copy(c, j, wown.at[j], wown_sem.at[j])

    tok_loads[0].start()
    far_copy(0).start()

    barrier = pltpu.get_barrier_semaphore()
    line = [lax.rem(ex + k, 4) * 8 + lax.rem(s, 8) for k in range(1, 4)]
    for z in (up, down):
        pl.semaphore_signal(barrier, inc=1, device_id=(s, z), device_id_type=MESH)
    for d in line + [ex * 8 + lax.rem(s + k, 8) for k in range(1, 8)]:
        pl.semaphore_signal(barrier, inc=1, device_id=(d, c), device_id_type=MESH)

    def z2_copy(j, half):
        half_rows = pl.ds(half * HALF, HALF)
        return pltpu.make_async_remote_copy(
            z2s.at[j, half_rows], z2r.at[j, half_rows], z2s_sem.at[j, half], z2r_sem.at[j, half],
            device_id=(s, (up, down)[half]), device_id_type=MESH,
        )

    def z_copy(j, way):
        return pltpu.make_async_remote_copy(
            zs.at[way, j], zr.at[way, j], zs_sem.at[way, j], zr_sem.at[way, j],
            device_id=(s, (up, down)[way]), device_id_type=MESH,
        )

    def z_last(h, way):
        cols = pl.ds(pl.multiple_of(h * HW, HW), HW)
        return pltpu.make_async_remote_copy(
            zs.at[way, LAST, :, cols], zr.at[way, LAST, :, cols],
            zs_sem.at[way, LAST + h], zr_sem.at[way, LAST + h],
            device_id=(s, (up, down)[way]), device_id_type=MESH,
        )

    def block_send(src, dst, send_sem, recv_sem, d):
        pltpu.make_async_remote_copy(
            src, dst, send_sem, recv_sem, device_id=(d, c), device_id_type=MESH
        ).start()

    def send_filters():
        plane_each(
            lambda d, slot: block_send(fs.at[slot], fr.at[s], fs_sem.at[0], fr_sem.at[0], d)
        )
        fr[s] = fs[me]

    def send_mixed(j, h):
        def one(d, slot):
            block_send(xs.at[j, slot], xr.at[j, s], xs_sem.at[j], xr_sem.at[j], d)

        plane_half(one, h)

        @pl.when(core == h)
        def _():
            xr[j, s] = xs[j, me]

        @pl.when(core != h)
        def _():
            one(s + 1 - 2 * core, h * CHIPS + s // 2)

    def send_conv(j):
        plane_each(
            lambda d, slot: block_send(
                ys.at[j, d], yr.at[j, me], ys_sem.at[j], yr_sem.at[j, core], d
            )
        )
        yr[j, me] = ys[j, s]

    def block_wait(buf, send_sem, recv_sem, count):
        part = buf.at[pl.ds(0, count)]
        return pltpu.make_async_remote_copy(
            part, part, send_sem, recv_sem, device_id=(s, c), device_id_type=MESH
        )

    def to_blocks(values, h):
        for a in range(OWN_A):
            part = values[a * N1 : (a + 1) * N1].T.reshape(CHIPS, CD, N1)
            bounce[h, :, a * CD : (a + 1) * CD, :] = part
        return bounce[h].astype(BF16)

    def half(j, h):
        return pl.ds(pl.multiple_of(j * CW + h * HW, HW), HW)

    def by_core(h):
        return pl.ds(h * CHIPS, CHIPS)

    def project_far(j, carry):
        far_copy(j).wait()
        z2s[j] = jnp.dot(tok[...], wfar[j], preferred_element_type=F32).astype(BF16)

        @pl.when(j < LAST)
        def _():
            z2_copy(j, 0).start()
            z2_copy(j, 1).start()

        return carry

    def project_near(j, carry):
        for way in range(2):
            near_copy(way, j).wait()
            part = jnp.dot(tok[...], wnear[way, lax.rem(j, 2)], preferred_element_type=F32)

            @pl.when(j + 2 < NC)
            def _():
                near_copy(way, j + 2).start()

            mine, other = pl.ds(way * HALF, HALF), pl.ds((1 - way) * HALF, HALF)
            z2_copy(j, way).wait_recv()
            zs[way, j, other] = part[(1 - way) * HALF : (2 - way) * HALF].astype(BF16)
            zs[way, j, mine] = (
                part[way * HALF : (way + 1) * HALF] + z2r[j, mine].astype(F32)
            ).astype(BF16)

            @pl.when(j == 0)
            def _():
                z_copy(0, way).start()

        return carry

    def start_sums(copy, j):
        for way in range(2):
            copy(j, way).start()

    def project_own(j, carry):
        own_copy(j).wait()
        own[j] = jnp.dot(tok[...], wown[j], preferred_element_type=F32)
        return carry

    def block_filters(j, carry):
        rows_of = pl.ds(pl.multiple_of(j * BR, BR), BR)
        for h in range(2):
            fs[by_core(h), rows_of] = to_blocks(fl[:, half(j, h)].astype(F32), h)
        return carry

    tok_loads[0].wait()
    far_copy(0).wait()
    tok_loads[1].start()
    far_copy(1).start()
    loads[2].start()
    for h in range(2):
        if h:
            tok_loads[1].wait()
        top = pl.ds(h * HALF, HALF)
        z2s[0, top] = jnp.dot(tok[top], wfar[0], preferred_element_type=F32).astype(BF16)
        if not h:
            pl.semaphore_wait(barrier, 12)
        z2_copy(0, h).start()
        if not h:
            for d in line:
                pl.semaphore_signal(line_sem, inc=1, device_id=(d, c), device_id_type=MESH)
    for way in range(2):
        near_copy(way, 0).start()
    for j in range(2, NC):
        far_copy(j).start()
    lax.fori_loop(1, 2, project_far, 0)
    for way in range(2):
        near_copy(way, 1).start()
    for i in (0, 3, 4, 5, 8):
        loads[i].start()
    loads[2].wait()
    lax.fori_loop(0, NC, block_filters, 0)
    pl.semaphore_wait(line_sem, 3)
    send_filters()
    for j in range(NC):
        own_copy(j).start()
    for i in (1, 6, 7):
        loads[i].start()
    lax.fori_loop(0, 2, project_near, 0)
    lax.fori_loop(2, 3, project_far, 0)
    lax.fori_loop(0, NC, project_own, 0)
    start_sums(z_copy, 1)
    lax.fori_loop(LAST, NC, project_far, 0)
    for i in (0, 1, 3, 4, 5, 6, 7, 8):
        loads[i].wait()

    def column(i):
        return pl.ds(i * N1, N1)

    def forward():
        for i in range(CD):
            pos[:, column(i)] = lanes[pl.ds(i, N1, stride=CD), :].astype(BF16)
        first[...] = jnp.dot(fwd[...], pos[...], preferred_element_type=F32)
        for i in range(CD):
            re, im = first[:N1, column(i)], first[N1:, column(i)]
            rows[column(i), :N1] = (re * tw[0] - im * tw[1]).astype(BF16)
            rows[column(i), N1:] = (re * tw[1] + im * tw[0]).astype(BF16)
        return jnp.dot(rows[...], mid[...], preferred_element_type=F32)

    def load_lanes(src, j):
        lanes[...] = src[j].astype(F32).reshape(SEQ * BR, N1)

    def transform_filters(j, carry):
        load_lanes(fr, (slice(None), pl.ds(pl.multiple_of(j * BR, BR), BR)))
        spec[j] = forward()
        return carry


    def gather_sums(j, h):
        cols = slice(h * HW, (h + 1) * HW)
        value = own[j, :, cols] + zr[0, j, :, cols].astype(F32) + zr[1, j, :, cols].astype(F32)
        mix = (gk[:, half(j, h)].astype(F32) * value).astype(BF16)
        mixed[:, half(j, h)] = mix
        xs[j, by_core(h)] = to_blocks(mix.astype(F32), h)
        send_mixed(j, h)

    def convolve(j):
        block_wait(xr.at[j], xs_sem.at[j], xr_sem.at[j], SEQ - 1).wait_recv()
        load_lanes(xr, j)
        second[...] = forward()
        for i in range(CD):
            re, im = second[column(i), :N1], second[column(i), N1:]
            fre, fim = spec[j, column(i), :N1], spec[j, column(i), N1:]
            rows[column(i), :N1] = (re * fre - im * fim).astype(BF16)
            rows[column(i), N1:] = (re * fim + im * fre).astype(BF16)
        second[...] = jnp.dot(rows[...], midi[...], preferred_element_type=F32)
        for i in range(CD):
            re, im = second[column(i), :N1], second[column(i), N1:]
            back[:N1, column(i)] = (re * tw[0] + im * tw[1]).astype(BF16)
            back[N1:, column(i)] = (im * tw[0] - re * tw[1]).astype(BF16)
        conv = jnp.dot(inv[...], back[...], preferred_element_type=F32)
        for i in range(CD):
            turns[pl.ds(i, N1, stride=CD), :] = conv[:, i * N1 : (i + 1) * N1]
        ys[j] = turns[...].reshape(SEQ, BR, N1).astype(BF16)
        send_conv(j)

    def finalize(j, h):
        @pl.when(core == h)
        def _():
            block_wait(yr.at[j], ys_sem.at[j], yr_sem.at[j, h], CHIPS - 1).wait_recv()

        @pl.when(core != h)
        def _():
            block_wait(yr.at[j], ys_sem.at[j], yr_sem.at[j, h], CHIPS).wait_recv()

        bounce[h] = yr[j, by_core(h)].astype(F32)
        for a in range(OWN_A):
            conv = bounce[h, :, a * CD : (a + 1) * CD, :].reshape(HW, N1).T
            here = pl.ds(a * N1, N1)
            total = conv + skip[:, half(j, h)] * mixed[here, half(j, h)].astype(F32)
            out[here, half(j, h)] = (gq[here, half(j, h)].astype(F32) * total).astype(BF16)

    def gather_chunk(j):
        z_copy(j, 0).wait_recv()
        z_copy(j, 1).wait_recv()
        gather_sums(j, 0)
        gather_sums(j, 1)

    def finish(j, carry):
        finalize(j, 0)
        finalize(j, 1)
        return carry

    def gather_last(h):
        z_last(h, 0).wait_recv()
        z_last(h, 1).wait_recv()
        gather_sums(LAST, h)

    gather_chunk(0)
    start_sums(z2_copy, LAST)
    lax.fori_loop(2, 3, project_near, 0)
    start_sums(z_copy, 2)
    block_wait(fr, fs_sem.at[0], fr_sem.at[0], SEQ - 1).wait_recv()
    lax.fori_loop(0, NC, transform_filters, 0)
    convolve(0)
    gather_chunk(1)
    lax.fori_loop(3, 4, project_near, 0)
    start_sums(z_last, 0)
    gather_chunk(2)
    start_sums(z_last, 1)
    convolve(1)
    gather_last(0)
    gather_last(1)
    convolve(2)
    lax.fori_loop(0, 2, finish, 0)
    convolve(3)
    lax.fori_loop(2, 4, finish, 0)

    def drain(j, carry):
        for h in range(2):
            z2_copy(j, h).wait_send()

            @pl.when(j < LAST)
            def _():
                z_copy(j, h).wait_send()

        block_wait(xr.at[j], xs_sem.at[j], xr_sem.at[j], SEQ - 1).wait_send()
        block_wait(yr.at[j], ys_sem.at[j], yr_sem.at[j, 0], SEQ - 1).wait_send()
        return carry

    for h in range(2):
        for way in range(2):
            z_last(h, way).wait_send()
    block_wait(fr, fs_sem.at[0], fr_sem.at[0], SEQ - 1).wait_send()
    lax.fori_loop(0, NC, drain, 0)


def local(tokens, w_in, gate_k, gate_q, filters, skip):
    any_spec = pl.BlockSpec(memory_space=pl.ANY)
    vm = pltpu.VMEM
    dma = pltpu.SemaphoreType.DMA
    block = (NC, SEQ, BR, N1)
    scratch = [
        vm((ROWS, FEAT), BF16), vm((NC, FEAT, CW), BF16), vm((2, 2, FEAT, CW), BF16), vm((NC, FEAT, CW), BF16),
        vm((ROWS, WIDTH), BF16), vm((ROWS, WIDTH), BF16), vm((ROWS, WIDTH), BF16), vm((1, WIDTH), F32),
        vm((2 * N1, N1), BF16), vm((2 * N1, 2 * N1), BF16), vm((2 * N1, 2 * N1), BF16),
        vm((N1, 2 * N1), BF16), vm((2, N1, N1), F32),
        vm((NC, ROWS, CW), BF16), vm((NC, ROWS, CW), BF16),
        vm((2, NC, ROWS, CW), BF16), vm((2, NC, ROWS, CW), BF16), vm((NC, ROWS, CW), F32),
        vm((ROWS, WIDTH), BF16),
        vm((SEQ, NC * BR, N1), BF16), vm((SEQ, NC * BR, N1), BF16),
        vm(block, BF16), vm(block, BF16), vm(block, BF16), vm(block, BF16),
        vm((2, CHIPS, BR, N1), F32), vm((SEQ * BR, N1), F32), vm((SEQ * BR, N1), F32), vm((NC, CD * N1, 2 * N1), F32),
        vm((N1, CD * N1), BF16), vm((2 * N1, CD * N1), F32), vm((CD * N1, 2 * N1), BF16),
        vm((CD * N1, 2 * N1), F32), vm((2 * N1, CD * N1), BF16),
        pltpu.SemaphoreType.REGULAR, dma((2,)), dma((9,)), dma((NC,)), dma((2, 2)), dma((NC,)),
        dma((NC, 2)), dma((NC, 2)), dma((2, NC + 1)), dma((2, NC + 1)),
        dma((1,)), dma((1,)), dma((NC,)), dma((NC,)), dma((NC,)), dma((NC, 2)),
    ]
    return pl.pallas_call(
        kernel,
        out_shape=pltpu.VMEM((ROWS, WIDTH), BF16),
        in_specs=[any_spec] * 11,
        out_specs=pl.BlockSpec(memory_space=pltpu.VMEM),
        scratch_shapes=scratch,
        compiler_params=pltpu.CompilerParams(
            collective_id=0, has_side_effects=True, vmem_limit_bytes=56 * 2**20
        ),
        name="hyena_block",
    )(tokens, w_in, gate_k, gate_q, filters, skip.reshape(1, WIDTH), *tables())


def solution(mesh):
    in_specs = (
        P("seq", "chan"),
        P("chan", None),
        P("seq", "chan"),
        P("seq", "chan"),
        P("seq", "chan"),
        P("chan"),
    )
    out_specs = P("seq", "chan")
    return jax.shard_map(local, mesh=mesh, in_specs=in_specs, out_specs=out_specs, check_vma=False)
```
